32 devices in a mesh: doc: 8 (over z, y), ctx: 4 (over x, core).
Axes of the slice: x: 2, y: 2, z: 4, core: 2. Of those that a mesh axis runs over, the one named last changes fastest.
Arguments:
- tokens: bfloat16 [8, 1024, 5120], P('doc', 'ctx'), may hold values from -640 to 640
- latents: float32 [16, 512], replicated, may hold values from -6 to 6
- w_keys: bfloat16 [5120, 512], replicated, may hold values from -0.078125 to 0.078125
- w_values: bfloat16 [5120, 512], replicated, may hold values from -0.078125 to 0.078125
- w_out: bfloat16 [512, 512], replicated, may hold values from -0.25 to 0.25
- latent_gain: float32 [512], replicated, may hold values from 0.1 to 1.9
- heads_down: bfloat16 [32, 512, 5120], P(('doc', 'ctx')), may hold values from -0.25 to 0.25
- heads_up: bfloat16 [32, 512, 5120], P(('doc', 'ctx')), may hold values from -0.25 to 0.25
- owner: int32 [32], replicated, may hold values from 0 to 31, each once
- requests: bfloat16 [6144, 5120], P(('doc', 'ctx')), may hold values from -6 to 6
- req_doc: int32 [6144], P(('doc', 'ctx')), may hold values from 0 to 7
- req_module: int32 [6144, 1], P(('doc', 'ctx')), may hold values from 0 to 31; in each aligned block of 192 rows (0 to 191, 192 to 383, ...) at most 7 rows name the same one
Outputs:
- adapted: bfloat16 [6144, 5120], P(('doc', 'ctx'))
The draws below stay inside these ranges and needn't reach their ends.
Inputs may be any that keep to these rules, and one draw needn't show every extreme that they name: Module m's heads are head slot owner[m]; every slot is named once. `req_module`: the 192 request rows of one device name any one module at most 7 times, and in every draw some device names some module exactly 7 times.
All inputs are finite; a program needn't handle non-finite values.
Results may differ from the reference program's by a relative error of at most 0.012.
The reference program's roundings to bfloat16 on the way (of `key_rows`, `value_rows`, `queries`, `attended`, `summary`, `coeff` and `update`) count: a program that leaves them out, or rounds other values in their place, can miss the bound.
Values may be sent and summed in bfloat16 or wider, within the bound.
No kernel may reach another device: no remote copies, remote signals or barrier semaphores. Data moves between devices by JAX's collectives and lax.ppermute only.
A program may use at most 128 MiB of HBM per device.

```python
import math
import jax
import jax.numpy as jnp
import numpy as np
from jax import lax

D = 5120
LAT = 16
HEADS = 4
HEAD_DIM = 128
LW = 512
REQ = 192
DOCS = 8
TOKENS = 1024
MODULES = 32
CAP = 7
N_DOC = 8
N_CTX = 4
DEVICES = 32


def draw_tokens(key, part):
    key_base = jax.random.fold_in(jax.random.fold_in(key, 17), 0)
    drawn = jnp.clip(jax.random.normal(key_base, (DOCS, TOKENS, D), jnp.float32), -4.0, 4.0)
    return drawn.astype(jnp.bfloat16)


def set_ends(entries, key, smallest, top_value):
    longest = entries.shape.index(max(entries.shape))
    spots = []
    for shift in (0, 1):
        where = [jax.random.randint(jax.random.fold_in(key, axis), (), 0, length) for axis, length in enumerate(entries.shape)]
        where[longest] = (where[longest] + shift) % entries.shape[longest]
        spots.append(tuple(where))
    return entries.at[spots[0]].set(smallest).at[spots[1]].set(top_value)


def block_scale(stream_key, shape, cuts, smallest, top_value):
    level, own = 1.0, jax.random.fold_in(stream_key, 6)
    for position, blocks in cuts:
        heights = jnp.exp(jax.random.uniform(jax.random.fold_in(own, position), (blocks,), jnp.float32, smallest / len(cuts), top_value / len(cuts)))
        level = level * jnp.repeat(heights, shape[position] // blocks).reshape([-1 if axis == position else 1 for axis in range(len(shape))])
    return level


def shared_out(own_key, own, number, rows, amount, top, bound, slope):
    order = jax.random.permutation(own_key, amount)
    crowded, usual = shares(amount, rows * top, bound, slope, True), shares(amount, rows * top, bound, slope, False)
    places = jnp.arange(amount)

    def named(sizes, turn):
        used = int((sizes > 0).sum())
        fixed = max(1, used // 4)
        passed = fixed + (places - fixed + turn * (used - fixed)) % max(1, amount - fixed)
        return jnp.zeros((amount,), jnp.int32).at[order[jnp.where(places < fixed, places, passed)]].set(jnp.asarray(sizes, jnp.int32))

    sizes = jnp.where(number % 4 == 0, named(crowded, number // 4), named(usual, number - number // 4 - 1))
    mixed = jax.random.permutation(jax.random.fold_in(own, 3), amount)
    source_of, receiver = mixed[0:amount // 2 * 2:2], mixed[1:amount // 2 * 2:2]
    margin = jnp.minimum(sizes[source_of] - 1, bound - sizes[receiver]) // 2
    margin = jnp.where((source_of == order[0]) | (receiver == order[0]) | (sizes[receiver] == 0), 0, jnp.maximum(margin, 0))
    passed = jax.random.randint(jax.random.fold_in(own, 4), (amount // 2,), 0, 1 << 20) % (margin + 1)
    sizes = sizes.at[source_of].add(-passed).at[receiver].add(passed)
    labels = jnp.searchsorted(jnp.cumsum(sizes), jnp.arange(rows * top), side="right").astype(jnp.int32)
    grid = labels.reshape(top, rows).T
    grid = grid[jax.random.permutation(jax.random.fold_in(own, 1), rows)]
    turn = jax.random.randint(jax.random.fold_in(own, 2), (rows, 1), 0, top)
    return jnp.take_along_axis(grid, (jnp.arange(top)[None, :] + turn) % top, axis=1)


def shares(number_of, total, limit, slope, full):
    loads = [(1 << 20) // math.isqrt(grade ** slope) + 1 for grade in range(1, number_of + 1)]
    largest = limit if full else min(limit, max(-(-total // number_of), total * loads[0] // sum(loads)))
    least = 1 if total - largest >= number_of - 1 else 0
    given, surplus = [largest] + [least] * (number_of - 1), total - largest - least * (number_of - 1)
    while surplus > 0:
        candidates = [i for i in range(1, number_of) if given[i] < largest] or [i for i in range(1, number_of) if given[i] < limit]
        whole, budget = sum([loads[i] for i in candidates]), surplus
        for i in candidates:
            more = min(limit - given[i], max(1, budget * loads[i] // whole), surplus)
            given[i] = given[i] + more
            surplus = surplus - more
    return np.array(given)


def bell_draw(own_key, dims, deviation, limit, pieces=(), held_as=jnp.bfloat16):
    result = jax.random.normal(own_key, dims, jnp.float32) * deviation
    if len(pieces) > 0:
        result = block_scale(own_key, dims, pieces, -0.22, 0.18) * result
    return jnp.clip(result, min=-limit, max=limit).astype(held_as)


def setup_inputs(seed: int = 0) -> dict:
    key_list = jax.random.split(jax.random.key(seed), 13)
    tokens = draw_tokens(jax.random.fold_in(key_list[12], 71), 0)
    latents = bell_draw(key_list[1], (LAT, LW), 1.0, 6.0, (), jnp.float32)
    w_keys = bell_draw(key_list[2], (D, LW), D ** -0.5, 0.078125)
    w_values = bell_draw(key_list[3], (D, LW), D ** -0.5, 0.078125)
    w_out = bell_draw(key_list[4], (LW, LW), LW ** -0.5, 0.25)
    latent_gain = jnp.clip(1.0 + 0.18 * jax.random.normal(key_list[5], (LW,), jnp.float32), 0.1, 1.9)
    heads_down = bell_draw(key_list[6], (MODULES, LW, D), LW ** -0.5, 0.25, ((0, 32),))
    heads_up = bell_draw(key_list[7], (MODULES, LW, D), LW ** -0.5, 0.25, ((0, 32),))
    owner = jax.random.permutation(key_list[8], MODULES).astype(jnp.int32)
    requests = bell_draw(key_list[9], (DEVICES * REQ, D), 1.0, 6.0, ((0, 32),))
    req_doc = set_ends(jax.random.randint(key_list[10], (DEVICES * REQ,), 0, DOCS), jax.random.fold_in(key_list[10], 1), 0, DOCS - 1).astype(jnp.int32)
    req_module_keys = jax.random.split(jax.random.fold_in(key_list[11], 1), (DEVICES * REQ) // REQ)
    req_module_turns = jax.random.permutation(jax.random.fold_in(key_list[11], 3), (DEVICES * REQ) // REQ)
    req_module = jax.vmap(lambda own, number: shared_out(jax.random.fold_in(key_list[11], 2), own, number, REQ, MODULES, 1, CAP, 2))(req_module_keys, req_module_turns).reshape((DEVICES * REQ, 1))
    return dict(tokens=tokens, latents=latents, w_keys=w_keys, w_values=w_values, w_out=w_out, latent_gain=latent_gain, heads_down=heads_down, heads_up=heads_up, owner=owner, requests=requests, req_doc=req_doc, req_module=req_module)


def apply_rows(picked_rows, tags, down_factor, up_factor):
    coeff = lax.dot_general(picked_rows, down_factor, (((1,), (1,)), ((), ())), preferred_element_type=jnp.float32) / math.sqrt(D)
    column_doc = jnp.arange(down_factor.shape[0], dtype=jnp.int32) // LAT
    matched = tags[:, None] - 1 == column_doc[None, :]
    coeff = jnp.where(matched, coeff, 0.0).astype(jnp.bfloat16)
    return (jnp.dot(coeff, up_factor, preferred_element_type=jnp.float32) / math.sqrt(LAT)).astype(jnp.bfloat16)

def reference(tokens, latents, w_keys, w_values, w_out, latent_gain, heads_down, heads_up, owner, requests, req_doc, req_module):
    flat_tokens = tokens.reshape(DOCS * TOKENS, D)
    key_rows = jnp.dot(flat_tokens, w_keys, preferred_element_type=jnp.float32).astype(jnp.bfloat16)
    value_rows = jnp.dot(flat_tokens, w_values, preferred_element_type=jnp.float32).astype(jnp.bfloat16)
    key_rows = key_rows.astype(jnp.float32).reshape(DOCS, TOKENS, HEADS, HEAD_DIM)
    value_rows = value_rows.astype(jnp.float32).reshape(DOCS, TOKENS, HEADS, HEAD_DIM)
    queries = latents.astype(jnp.bfloat16).astype(jnp.float32).reshape(LAT, HEADS, HEAD_DIM)
    scores = jnp.einsum('ihe,dthe->dhit', queries, key_rows, precision=lax.Precision.HIGHEST) / math.sqrt(HEAD_DIM)
    probs = jax.nn.softmax(scores, axis=-1)
    attended = jnp.einsum('dhit,dthe->dihe', probs, value_rows, precision=lax.Precision.HIGHEST)
    attended = attended.reshape(DOCS * LAT, LW).astype(jnp.bfloat16)
    mixed_state = latents.reshape(1, LAT, LW) + jnp.dot(attended, w_out, preferred_element_type=jnp.float32).reshape(DOCS, LAT, LW)
    summary = mixed_state * lax.rsqrt(lax.optimization_barrier(jnp.mean(mixed_state * mixed_state, axis=-1, keepdims=True)) + 1e-06) * latent_gain
    summary = summary.astype(jnp.bfloat16).reshape(DOCS * LAT, LW)
    devices = N_DOC * N_CTX
    blocks = req_module[:, 0].reshape(devices, REQ)
    block_docs = req_doc.reshape(devices, REQ)

    def per_module(module, total):
        slot = owner[module]
        down_factor = jnp.dot(summary, heads_down[slot], preferred_element_type=jnp.float32).astype(jnp.bfloat16)
        up_factor = jnp.dot(summary, heads_up[slot], preferred_element_type=jnp.float32).astype(jnp.bfloat16)
        order = jnp.argsort(jnp.where(blocks == module, 0, 1), axis=1, stable=True)[:, :CAP].astype(jnp.int32)
        picked = jnp.take_along_axis(blocks, order, axis=1)
        valid = (picked == module).reshape(-1)
        global_rows = (jnp.arange(devices, dtype=jnp.int32)[:, None] * REQ + order).reshape(-1)
        tags = jnp.where(valid, jnp.take_along_axis(block_docs, order, axis=1).reshape(-1) + 1, 0)
        update = apply_rows(requests[global_rows], tags, down_factor, up_factor)
        return total.at[global_rows].add(jnp.where(valid[:, None], update.astype(jnp.float32), 0.0))
    total = lax.fori_loop(0, MODULES, per_module, jnp.zeros((devices * REQ, D), jnp.float32))
    return (requests.astype(jnp.float32) + total).astype(jnp.bfloat16)
```

```python
import functools
import math

import jax
import jax.numpy as jnp
from jax import lax
from jax.experimental import pallas as pl
from jax.experimental.pallas import tpu as pltpu
from jax.sharding import PartitionSpec as P

HEADS = 4
SUB = 8
LANES = 128
ALL = ("doc", "ctx")


def compiler_params():
    return pltpu.CompilerParams(vmem_limit_bytes=48 * 1024 * 1024)


def scatter_pieces(stage, piece_index, values, blocks, capacity, piece):
    for slot in range(capacity):
        for lane in range(piece // LANES):
            stage[
                slot * (piece // LANES) + lane, pl.ds(piece_index, blocks, stride=SUB), :
            ] = values[slot * blocks : (slot + 1) * blocks, lane * LANES : (lane + 1) * LANES]


def gather_pieces(stage, piece_index, blocks, capacity, piece):
    return jnp.concatenate(
        [
            jnp.concatenate(
                [
                    stage[slot * (piece // LANES) + lane, pl.ds(piece_index, blocks, stride=SUB), :]
                    for lane in range(piece // LANES)
                ],
                axis=1,
            ).astype(jnp.bfloat16)
            for slot in range(capacity)
        ],
        axis=0,
    )


def fill_stage(stage, source):
    for lane in range(stage.shape[0]):
        stage[lane] = source[:, lane * LANES : (lane + 1) * LANES].astype(jnp.float32)


def drain_stage(stage, target):
    for lane in range(stage.shape[0]):
        target[:, lane * LANES : (lane + 1) * LANES] = stage[lane].astype(target.dtype)


def slot_of_rows(module_column, module_row, owner_column, blocks):
    rows = module_row.shape[1]
    module_ids = lax.broadcasted_iota(jnp.int32, (blocks, rows), 0)
    target = jnp.sum(
        jnp.where(module_ids == module_row, owner_column, 0), axis=0, keepdims=True
    )
    first = lax.broadcasted_iota(jnp.int32, (rows, rows), 0)
    second = lax.broadcasted_iota(jnp.int32, (rows, rows), 1)
    earlier = (module_column == module_row) & (first < second)
    rank = jnp.sum(earlier.astype(jnp.int32), axis=0, keepdims=True)
    return rank * blocks + target


def place_kernel(
    blocks, capacity, module_column, module_row, owner_column, doc_row, requests, sent, tags, slots, stage
):
    rows, width = requests.shape
    piece = width // SUB
    slot_row = slot_of_rows(module_column[...], module_row[...], owner_column[...], blocks)
    slots[...] = slot_row
    placed = lax.broadcasted_iota(jnp.int32, (capacity * blocks, rows), 0) == slot_row
    tags[...] = jnp.sum(
        jnp.where(placed, doc_row[...] + 1, 0), axis=1, keepdims=True
    )
    placer = placed.astype(jnp.float32).astype(jnp.bfloat16)
    for index in range(SUB):
        moved = jnp.dot(
            placer,
            requests[:, index * piece : (index + 1) * piece],
            preferred_element_type=jnp.float32,
        )
        scatter_pieces(stage, index, moved, blocks, capacity, piece)
    drain_stage(stage, sent)


def apply_kernel(blocks, capacity, latent_count, arrived, tags, column_doc, down, up, update, stage):
    width = down.shape[1]
    piece = width // SUB
    fill_stage(stage, arrived)
    coeff = None
    for index in range(SUB):
        part = lax.dot_general(
            gather_pieces(stage, index, blocks, capacity, piece),
            down[:, index * piece : (index + 1) * piece],
            (((1,), (1,)), ((), ())),
            preferred_element_type=jnp.float32,
        )
        coeff = part if coeff is None else coeff + part
    matched = tags[...] - 1 == column_doc[...]
    coeff = jnp.where(matched, coeff * (1.0 / math.sqrt(width)), 0.0).astype(jnp.bfloat16)
    for index in range(SUB):
        moved = jnp.dot(
            coeff, up[:, index * piece : (index + 1) * piece], preferred_element_type=jnp.float32
        ) * (1.0 / math.sqrt(latent_count))
        scatter_pieces(stage, index, moved, blocks, capacity, piece)
    drain_stage(stage, update)


def finish_kernel(blocks, capacity, returned, slots, requests, adapted, stage):
    rows, width = requests.shape
    piece = width // SUB
    fill_stage(stage, returned)
    placed = lax.broadcasted_iota(jnp.int32, (capacity * blocks, rows), 0) == slots[...]
    placer = placed.astype(jnp.float32).astype(jnp.bfloat16)
    for index in range(SUB):
        gathered = lax.dot_general(
            placer,
            gather_pieces(stage, index, blocks, capacity, piece),
            (((0,), (0,)), ((), ())),
            preferred_element_type=jnp.float32,
        )
        columns = slice(index * piece, (index + 1) * piece)
        adapted[:, columns] = (requests[:, columns].astype(jnp.float32) + gathered).astype(
            adapted.dtype
        )


def on_device(
    tokens,
    latents,
    w_keys,
    w_values,
    w_out,
    latent_gain,
    heads_down,
    heads_up,
    owner,
    requests,
    req_doc,
    req_module,
):
    doc_count = lax.axis_size("doc")
    ctx_count = lax.axis_size("ctx")
    blocks = doc_count * ctx_count
    rows, width = requests.shape
    capacity = max(2, rows // blocks + 1)
    piece = width // SUB
    latent_count, latent_width = latents.shape
    head_dim = latent_width // HEADS
    my_doc = lax.axis_index("doc")
    my_ctx = lax.axis_index("ctx")
    stage = pltpu.VMEM((capacity * piece // LANES, blocks * SUB, LANES), jnp.float32)
    block_shape = jax.ShapeDtypeStruct((blocks * SUB, capacity * piece), jnp.bfloat16)

    def exchange(values):
        return lax.all_to_all(
            values.reshape(blocks, SUB, capacity * piece), ALL, split_axis=0, concat_axis=0, tiled=True
        ).reshape(blocks * SUB, capacity * piece)

    sent, tags, slots = pl.pallas_call(
        functools.partial(place_kernel, blocks, capacity),
        out_shape=(
            block_shape,
            jax.ShapeDtypeStruct((capacity * blocks, 1), jnp.int32),
            jax.ShapeDtypeStruct((1, rows), jnp.int32),
        ),
        scratch_shapes=[stage],
        compiler_params=compiler_params(),
        name="place_rows",
    )(req_module, req_module.reshape(1, rows), owner.reshape(blocks, 1), req_doc.reshape(1, rows), requests)
    arrived = exchange(sent)

    local_tokens = tokens[0]
    key_rows = jnp.dot(local_tokens, w_keys, preferred_element_type=jnp.float32).astype(jnp.bfloat16)
    value_rows = jnp.dot(local_tokens, w_values, preferred_element_type=jnp.float32).astype(
        jnp.bfloat16
    )
    queries = latents.astype(jnp.bfloat16).reshape(latent_count, HEADS, head_dim)
    scores = jnp.einsum(
        "ihe,the->hit",
        queries,
        key_rows.reshape(-1, HEADS, head_dim),
        preferred_element_type=jnp.float32,
    ) / math.sqrt(head_dim)
    score_peak = jnp.max(scores, axis=-1)
    expo = jnp.exp(scores - score_peak[..., None])
    weight_sum = jnp.sum(expo, axis=-1)
    weighted = jnp.einsum(
        "hit,the->hie",
        expo,
        value_rows.astype(jnp.float32).reshape(-1, HEADS, head_dim),
        precision=lax.Precision.HIGHEST,
    )
    entries = HEADS * latent_count
    tag_count = capacity * blocks
    extra = jnp.concatenate(
        [score_peak.reshape(-1), weight_sum.reshape(-1), tags[:, 0].astype(jnp.float32)]
    )
    extra_rows = -(-extra.shape[0] // head_dim)
    extra = jnp.pad(extra, (0, extra_rows * head_dim - extra.shape[0])).reshape(extra_rows, head_dim)
    mine = jnp.concatenate([weighted.reshape(entries, head_dim), extra], axis=0)
    pieces = lax.all_gather(mine, "ctx")
    weighted = pieces[:, :entries]
    extra = pieces[:, entries:].reshape(ctx_count, -1)
    score_peak = extra[:, :entries]
    weight_sum = extra[:, entries : 2 * entries]
    ctx_tags = extra[:, 2 * entries : 2 * entries + tag_count]
    ratio = jnp.exp(score_peak - jnp.max(score_peak, axis=0, keepdims=True))
    total = jnp.sum(weight_sum * ratio, axis=0)
    weighted = jnp.sum(weighted * ratio[..., None], axis=0)
    attended = (
        (weighted / total[:, None])
        .reshape(HEADS, latent_count, head_dim)
        .transpose(1, 0, 2)
        .reshape(latent_count, latent_width)
        .astype(jnp.bfloat16)
    )
    mixed_state = latents + jnp.dot(attended, w_out, preferred_element_type=jnp.float32)
    summary = (
        mixed_state
        * lax.rsqrt(jnp.mean(mixed_state * mixed_state, axis=-1, keepdims=True) + 1e-06)
        * latent_gain
    ).astype(jnp.bfloat16)

    tag_rows = -(-(ctx_count * tag_count) // latent_width)
    flat_tags = ctx_tags.astype(jnp.bfloat16).reshape(-1)
    flat_tags = jnp.pad(flat_tags, (0, tag_rows * latent_width - flat_tags.shape[0]))
    packet = jnp.concatenate([summary, flat_tags.reshape(tag_rows, latent_width)], axis=0)
    share = doc_count // ctx_count
    fetched = []
    for turn in range(share):
        pairs = [
            (doc * ctx_count + ctx, (doc ^ (ctx * share + turn)) * ctx_count + ctx)
            for doc in range(doc_count)
            for ctx in range(ctx_count)
        ]
        fetched.append(lax.ppermute(packet, ALL, pairs))
    everyone = lax.all_gather(jnp.stack(fetched), "ctx").reshape(
        doc_count, latent_count + tag_rows, latent_width
    )
    summaries = everyone[:, :latent_count].reshape(doc_count * latent_count, latent_width)
    column_doc = (
        jnp.arange(doc_count * latent_count, dtype=jnp.int32)[None, :] // latent_count
    ) ^ my_doc
    all_tags = everyone[:, latent_count:].reshape(doc_count, -1)[:, : ctx_count * tag_count]
    all_tags = all_tags.reshape(doc_count, ctx_count, capacity, blocks)
    me = my_doc * ctx_count + my_ctx
    my_tags = jnp.sum(
        jnp.where(jnp.arange(blocks) == me, all_tags.astype(jnp.float32), 0.0), axis=-1
    )
    by_doc = jnp.arange(doc_count, dtype=jnp.int32)
    unmix = (by_doc[:, None] ^ my_doc) == by_doc[None, :]
    my_tags = jnp.sum(jnp.where(unmix[:, :, None, None], my_tags[None], 0.0), axis=1)
    my_tags = my_tags.transpose(2, 0, 1).reshape(tag_count, 1).astype(jnp.int32)

    down_factor = jnp.dot(summaries, heads_down[0], preferred_element_type=jnp.float32).astype(
        jnp.bfloat16
    )
    up_factor = jnp.dot(summaries, heads_up[0], preferred_element_type=jnp.float32).astype(
        jnp.bfloat16
    )
    update = pl.pallas_call(
        functools.partial(apply_kernel, blocks, capacity, latent_count),
        out_shape=block_shape,
        scratch_shapes=[stage],
        compiler_params=compiler_params(),
        name="apply_rows",
    )(arrived, my_tags, column_doc, down_factor, up_factor)
    returned = exchange(update)
    return pl.pallas_call(
        functools.partial(finish_kernel, blocks, capacity),
        out_shape=jax.ShapeDtypeStruct((rows, width), jnp.bfloat16),
        scratch_shapes=[stage],
        compiler_params=compiler_params(),
        name="finish_rows",
    )(returned, slots, requests)


def solution(mesh):
    in_specs = (
        P("doc", "ctx", None),
        P(),
        P(),
        P(),
        P(),
        P(),
        P(ALL, None, None),
        P(ALL, None, None),
        P(),
        P(ALL, None),
        P(ALL),
        P(ALL, None),
    )
    return jax.shard_map(
        on_device, mesh=mesh, in_specs=in_specs, out_specs=P(ALL, None), check_vma=False
    )
```

```python
import functools
import math

import jax
import jax.numpy as jnp
from jax import lax
from jax.experimental import pallas as pl
from jax.experimental.pallas import tpu as pltpu
from jax.sharding import PartitionSpec as P

HEADS = 4
SUB = 8
LANES = 128
VMEM_LIMIT = 60 * 1024 * 1024
ALL = ("doc", "ctx")


def call(kernel, name, **options):
    return pl.pallas_call(
        kernel,
        name=name,
        compiler_params=pltpu.CompilerParams(vmem_limit_bytes=VMEM_LIMIT),
        **options,
    )


def scatter_pieces(stage, piece_index, values, blocks, capacity, piece):
    for slot in range(capacity):
        for lane in range(piece // LANES):
            stage[
                slot * (piece // LANES) + lane, pl.ds(piece_index, blocks, stride=SUB), :
            ] = values[slot * blocks : (slot + 1) * blocks, lane * LANES : (lane + 1) * LANES]


def gather_pieces(stage, piece_index, blocks, capacity, piece):
    return jnp.concatenate(
        [
            jnp.concatenate(
                [
                    stage[slot * (piece // LANES) + lane, pl.ds(piece_index, blocks, stride=SUB), :]
                    for lane in range(piece // LANES)
                ],
                axis=1,
            ).astype(jnp.bfloat16)
            for slot in range(capacity)
        ],
        axis=0,
    )


def fill_stage(stage, sources):
    start = 0
    for source in sources:
        for lane in range(source.shape[1] // LANES):
            stage[start] = source[:, lane * LANES : (lane + 1) * LANES].astype(jnp.float32)
            start += 1


def drain_stage(stage, targets):
    start = 0
    for target in targets:
        for lane in range(target.shape[1] // LANES):
            target[:, lane * LANES : (lane + 1) * LANES] = stage[start].astype(target.dtype)
            start += 1


def as_column(row):
    n = row.shape[1]
    on_diagonal = lax.broadcasted_iota(jnp.int32, (n, n), 0) == lax.broadcasted_iota(
        jnp.int32, (n, n), 1
    )
    return jnp.sum(jnp.where(on_diagonal, row, jnp.zeros_like(row)), axis=1, keepdims=True)


def as_row(column):
    n = column.shape[0]
    on_diagonal = lax.broadcasted_iota(jnp.int32, (n, n), 0) == lax.broadcasted_iota(
        jnp.int32, (n, n), 1
    )
    return jnp.sum(jnp.where(on_diagonal, column, jnp.zeros_like(column)), axis=0, keepdims=True)


def place_kernel(
    blocks, capacity, owner_row, module_row, doc_row, requests, first_sent, second_sent, tags, slots, stage
):
    rows, width = requests.shape
    piece = width // SUB
    modules = module_row[...]
    owners = as_column(owner_row[...])
    named = lax.broadcasted_iota(jnp.int32, (blocks, rows), 0) == modules
    target = jnp.sum(jnp.where(named, owners, 0), axis=0, keepdims=True)
    first = lax.broadcasted_iota(jnp.int32, (rows, rows), 0)
    second = lax.broadcasted_iota(jnp.int32, (rows, rows), 1)
    ahead = (as_column(modules) == modules) & (first < second)
    rank = jnp.sum(ahead.astype(jnp.int32), axis=0, keepdims=True)
    slot_row = rank * blocks + target
    slots[...] = slot_row
    slot_column = as_column(slot_row)
    documents = as_column(doc_row[...] + 1)
    for part in range(tags.shape[0]):
        lanes = lax.broadcasted_iota(jnp.int32, (rows, LANES), 1) + part * LANES
        tags[part : part + 1, :] = jnp.sum(
            jnp.where(lanes == slot_column, documents, 0), axis=0, keepdims=True
        ).astype(jnp.float32)
    slot_ids = lax.broadcasted_iota(jnp.int32, (capacity * blocks, rows), 0)
    placer = (slot_ids == slot_row).astype(jnp.float32).astype(jnp.bfloat16)
    for index in range(SUB):
        moved = jnp.dot(
            placer,
            requests[:, index * piece : (index + 1) * piece],
            preferred_element_type=jnp.float32,
        )
        scatter_pieces(stage, index, moved, blocks, capacity, piece)
    drain_stage(stage, (first_sent, second_sent))


def attend_kernel(
    chunks, tokens, w_keys, w_values, latents, tags, partial, tokens_in, keys_in, values_in, done
):
    depth = w_keys.shape[0] // chunks
    copies = []
    for chunk in range(chunks):
        part = pl.ds(chunk * depth, depth)
        copies.append(
            [
                pltpu.make_async_copy(
                    tokens.at[0, :, part], tokens_in.at[chunk], done.at[chunk, 0]
                ),
                pltpu.make_async_copy(w_keys.at[part, :], keys_in.at[chunk], done.at[chunk, 1]),
                pltpu.make_async_copy(w_values.at[part, :], values_in.at[chunk], done.at[chunk, 2]),
            ]
        )
    for group in copies:
        for copy in group:
            copy.start()
    keys = values = 0.0
    for chunk in range(chunks):
        for copy in copies[chunk]:
            copy.wait()
        keys = keys + jnp.dot(
            tokens_in[chunk], keys_in[chunk], preferred_element_type=jnp.float32
        )
        values = values + jnp.dot(
            tokens_in[chunk], values_in[chunk], preferred_element_type=jnp.float32
        )
    latent_count, width = latents.shape
    head_dim = width // HEADS
    queries = latents[...].astype(jnp.bfloat16)
    key_rows = keys.astype(jnp.bfloat16)
    value_rows = values.astype(jnp.bfloat16).astype(jnp.float32)
    peaks, sums = [], []
    for head in range(HEADS):
        lanes = slice(head * head_dim, (head + 1) * head_dim)
        scores = lax.dot_general(
            queries[:, lanes],
            key_rows[:, lanes],
            (((1,), (1,)), ((), ())),
            preferred_element_type=jnp.float32,
        ) / math.sqrt(head_dim)
        peak = jnp.max(scores, axis=1, keepdims=True)
        expo = jnp.exp(scores - peak)
        peaks.append(peak)
        sums.append(jnp.sum(expo, axis=1, keepdims=True))
        partial[head * latent_count : (head + 1) * latent_count, :] = jnp.dot(
            expo,
            value_rows[:, lanes],
            precision=lax.Precision.HIGHEST,
            preferred_element_type=jnp.float32,
        )
    entries = HEADS * latent_count
    partial[entries:, :] = jnp.zeros_like(partial[entries:, :])
    partial[entries : entries + 1, :entries] = as_row(jnp.concatenate(peaks, axis=0))
    partial[entries + 1 : entries + 2, :entries] = as_row(jnp.concatenate(sums, axis=0))
    partial[entries + 2 : entries + 2 + tags.shape[0], :] = tags[...]


def summary_kernel(tag_parts, pieces, latents, w_out, gain, packet):
    members = pieces.shape[0]
    latent_count, width = latents.shape
    entries = HEADS * latent_count
    peaks = [as_column(pieces[c, entries : entries + 1, :entries]) for c in range(members)]
    summit = functools.reduce(jnp.maximum, peaks)
    total, weighted = 0.0, 0.0
    for c in range(members):
        ratio = jnp.exp(peaks[c] - summit)
        total = total + as_column(pieces[c, entries + 1 : entries + 2, :entries]) * ratio
        weighted = weighted + pieces[c, :entries, :] * ratio
    attended = weighted / total
    attended = jnp.concatenate(
        [attended[h * latent_count : (h + 1) * latent_count] for h in range(HEADS)], axis=1
    ).astype(jnp.bfloat16)
    mixed = latents[...] + jnp.dot(attended, w_out[...], preferred_element_type=jnp.float32)
    summary = (
        mixed
        * lax.rsqrt(jnp.mean(mixed * mixed, axis=1, keepdims=True) + 1e-06)
        * gain[...]
    )
    packet[:latent_count, :] = summary.astype(jnp.bfloat16)
    tag_rows = [
        jnp.concatenate(
            [pieces[c, entries + 2 + part : entries + 3 + part, :] for part in range(tag_parts)],
            axis=1,
        )
        for c in range(members)
    ]
    block = jnp.concatenate(tag_rows, axis=0)
    block = jnp.pad(
        block,
        ((0, packet.shape[0] - latent_count - members), (0, width - tag_parts * LANES)),
    )
    packet[latent_count:, :] = block.astype(jnp.bfloat16)


def factor_kernel(
    blocks,
    capacity,
    early,
    latent_count,
    chunks,
    me,
    everyone,
    heads_down,
    heads_up,
    down,
    up,
    tags_first,
    tags_second,
    heads_in,
    factors_out,
    arrived,
    left,
):
    depth = down.shape[1] // chunks
    jobs = []
    for chunk in range(chunks):
        part = pl.ds(chunk * depth, depth)
        for side, (heads, factor) in enumerate(((heads_down, down), (heads_up, up))):
            jobs.append(
                (
                    chunk,
                    side,
                    pltpu.make_async_copy(
                        heads.at[0, :, part], heads_in.at[chunk, side], arrived.at[chunk, side]
                    ),
                    pltpu.make_async_copy(
                        factors_out.at[chunk, side], factor.at[:, part], left.at[chunk, side]
                    ),
                )
            )
    for job in jobs:
        job[2].start()
    documents = everyone.shape[0]
    members = blocks // documents
    summaries = jnp.concatenate([everyone[x, :latent_count, :] for x in range(documents)], axis=0)
    device = me[0, 0]
    my_doc = device // members
    by_entry = jnp.concatenate(
        [everyone[x, latent_count:, :].astype(jnp.float32)[:members] for x in range(documents)],
        axis=0,
    ).astype(jnp.bfloat16)
    source = lax.broadcasted_iota(jnp.int32, (blocks, blocks), 0)
    entry = lax.broadcasted_iota(jnp.int32, (blocks, blocks), 1)
    sorter = source == ((entry // members) ^ my_doc) * members + entry % members
    sorter = sorter.astype(jnp.float32).astype(jnp.bfloat16)
    arranged = jnp.dot(sorter, by_entry, preferred_element_type=jnp.float32)
    lanes = lax.broadcasted_iota(jnp.int32, arranged.shape, 1)
    for slot in range(capacity):
        column = jnp.sum(
            jnp.where(lanes == slot * blocks + device, arranged, 0.0), axis=1, keepdims=True
        ).astype(jnp.int32)
        target, position = (tags_first, slot) if slot < early else (tags_second, slot - early)
        target[position * blocks : (position + 1) * blocks, :] = column
    for chunk, side, arriving, leaving in jobs:
        arriving.wait()
        factors_out[chunk, side] = jnp.dot(
            summaries, heads_in[chunk, side], preferred_element_type=jnp.float32
        ).astype(jnp.bfloat16)
        leaving.start()
    for job in jobs:
        job[3].wait()


def apply_kernel(blocks, capacity, latent_count, members, me, tags, down, up, arrived, *refs):
    *ready, update, stage = refs
    width = down.shape[1]
    piece = width // SUB
    fill_stage(stage, (arrived,))
    coeff = None
    for index in range(SUB):
        part = lax.dot_general(
            gather_pieces(stage, index, blocks, capacity, piece),
            down[:, index * piece : (index + 1) * piece],
            (((1,), (1,)), ((), ())),
            preferred_element_type=jnp.float32,
        )
        coeff = part if coeff is None else coeff + part
    column_doc = (
        lax.broadcasted_iota(jnp.int32, coeff.shape, 1) // latent_count
    ) ^ (me[0, 0] // members)
    matched = tags[...] - 1 == column_doc
    coeff = jnp.where(matched, coeff / math.sqrt(width), 0.0).astype(jnp.bfloat16)
    for index in range(SUB):
        moved = jnp.dot(
            coeff, up[:, index * piece : (index + 1) * piece], preferred_element_type=jnp.float32
        ) * (1.0 / math.sqrt(latent_count))
        scatter_pieces(stage, index, moved, blocks, capacity, piece)
    start = 0
    for part in ready:
        start = part.shape[1]
        update[:, :start] = part[...]
    drain_stage(stage, (update.at[:, start:],))


def finish_kernel(blocks, capacity, returned, slots, requests, adapted, stage):
    rows, width = requests.shape
    piece = width // SUB
    fill_stage(stage, (returned,))
    placed = lax.broadcasted_iota(jnp.int32, (capacity * blocks, rows), 0) == slots[...]
    placer = placed.astype(jnp.float32).astype(jnp.bfloat16)
    for index in range(SUB):
        gathered = lax.dot_general(
            placer,
            gather_pieces(stage, index, blocks, capacity, piece),
            (((0,), (0,)), ((), ())),
            preferred_element_type=jnp.float32,
        )
        columns = slice(index * piece, (index + 1) * piece)
        adapted[:, columns] = (requests[:, columns].astype(jnp.float32) + gathered).astype(
            adapted.dtype
        )


def on_device(
    tokens,
    latents,
    w_keys,
    w_values,
    w_out,
    latent_gain,
    heads_down,
    heads_up,
    owner,
    requests,
    req_doc,
    req_module,
):
    doc_count = lax.axis_size("doc")
    ctx_count = lax.axis_size("ctx")
    blocks = doc_count * ctx_count
    rows, width = requests.shape
    capacity = max(2, rows // blocks + 1)
    piece = width // SUB
    latent_count, latent_width = latents.shape
    head_dim = latent_width // HEADS
    my_doc = lax.axis_index("doc")
    my_ctx = lax.axis_index("ctx")
    early = max(1, (capacity - 1) // 2)
    late = capacity - early
    tag_parts = -(-(capacity * blocks) // LANES)
    me = (my_doc * ctx_count + my_ctx).astype(jnp.int32).reshape(1, 1)
    in_smem = pl.BlockSpec(memory_space=pltpu.SMEM)
    in_vmem = pl.BlockSpec(memory_space=pltpu.VMEM)
    in_hbm = pl.BlockSpec(memory_space=pl.ANY)

    def after(values, *others):
        return lax.optimization_barrier((values, *others))[0]

    def block_type(slot_count):
        return jax.ShapeDtypeStruct((blocks * SUB, slot_count * piece), jnp.bfloat16)

    def stage_type(slot_count):
        return pltpu.VMEM((slot_count * piece // LANES, blocks * SUB, LANES), jnp.float32)

    def exchange(values):
        return lax.all_to_all(
            values.reshape(blocks, SUB, -1), ALL, split_axis=0, concat_axis=0, tiled=True
        ).reshape(values.shape)

    first_sent, second_sent, tags, slots = call(
        functools.partial(place_kernel, blocks, capacity),
        "place_rows",
        out_shape=(
            block_type(early),
            block_type(late),
            jax.ShapeDtypeStruct((tag_parts, LANES), jnp.float32),
            jax.ShapeDtypeStruct((1, rows), jnp.int32),
        ),
        scratch_shapes=[stage_type(capacity)],
    )(
        owner.reshape(1, blocks),
        req_module.reshape(1, rows),
        req_doc.reshape(1, rows),
        requests,
    )
    first_arrived = exchange(first_sent)

    token_count = tokens.shape[1]
    entries = HEADS * latent_count
    partial_rows = -(-(entries + 2 + tag_parts) // SUB) * SUB
    chunks = width // (SUB * LANES)
    depth = width // chunks
    partial = call(
        functools.partial(attend_kernel, chunks),
        "attend",
        in_specs=[in_hbm] * 3 + [in_vmem] * 2,
        out_shape=jax.ShapeDtypeStruct((partial_rows, head_dim), jnp.float32),
        scratch_shapes=[
            pltpu.VMEM((chunks, token_count, depth), jnp.bfloat16),
            pltpu.VMEM((chunks, depth, latent_width), jnp.bfloat16),
            pltpu.VMEM((chunks, depth, latent_width), jnp.bfloat16),
            pltpu.SemaphoreType.DMA((chunks, 3)),
        ],
    )(tokens, w_keys, w_values, latents, tags)
    packet_rows = latent_count + 16
    packet = call(
        functools.partial(summary_kernel, tag_parts),
        "summarize",
        out_shape=jax.ShapeDtypeStruct((packet_rows, latent_width), jnp.bfloat16),
    )(lax.all_gather(partial, "ctx"), latents, w_out, latent_gain.reshape(1, latent_width))

    share = doc_count // ctx_count
    fetched = []
    for turn in range(share):
        pairs = [
            (doc * ctx_count + ctx, (doc ^ (ctx * share + turn)) * ctx_count + ctx)
            for doc in range(doc_count)
            for ctx in range(ctx_count)
        ]
        fetched.append(lax.ppermute(packet, ALL, pairs))
    second_arrived = exchange(after(second_sent, *fetched))
    everyone = lax.all_gather(jnp.stack(fetched), "ctx").reshape(
        doc_count, packet_rows, latent_width
    )

    def tag_type(slot_count):
        return jax.ShapeDtypeStruct((slot_count * blocks, 1), jnp.int32)

    factor_type = jax.ShapeDtypeStruct((doc_count * latent_count, width), jnp.bfloat16)
    down_factor, up_factor, first_tags, second_tags = call(
        functools.partial(factor_kernel, blocks, capacity, early, latent_count, chunks),
        "factors",
        in_specs=[in_smem, in_vmem, in_hbm, in_hbm],
        out_specs=(in_hbm, in_hbm, in_vmem, in_vmem),
        out_shape=(factor_type, factor_type, tag_type(early), tag_type(late)),
        scratch_shapes=[
            pltpu.VMEM((chunks, 2, latent_width, depth), jnp.bfloat16),
            pltpu.VMEM((chunks, 2, doc_count * latent_count, depth), jnp.bfloat16),
            pltpu.SemaphoreType.DMA((chunks, 2)),
            pltpu.SemaphoreType.DMA((chunks, 2)),
        ],
    )(me, everyone, heads_down, heads_up)

    def apply(tag_column, slot_count, arrived, *ready):
        total = slot_count + sum(part.shape[1] for part in ready) // piece
        return call(
            functools.partial(apply_kernel, blocks, slot_count, latent_count, ctx_count),
            "apply_rows",
            in_specs=[in_smem] + [in_vmem] * (4 + len(ready)),
            out_shape=block_type(total),
            scratch_shapes=[stage_type(slot_count)],
        )(me, tag_column, down_factor, up_factor, arrived, *ready)

    first_update = apply(first_tags, early, first_arrived)
    update = apply(second_tags, late, after(second_arrived, first_update), first_update)
    returned = exchange(update)
    return call(
        functools.partial(finish_kernel, blocks, capacity),
        "finish_rows",
        out_shape=jax.ShapeDtypeStruct((rows, width), jnp.bfloat16),
        scratch_shapes=[stage_type(capacity)],
    )(returned, slots, requests)


def solution(mesh):
    in_specs = (
        P("doc", "ctx", None),
        P(),
        P(),
        P(),
        P(),
        P(),
        P(ALL, None, None),
        P(ALL, None, None),
        P(),
        P(ALL, None),
        P(ALL),
        P(ALL, None),
    )
    return jax.shard_map(
        on_device, mesh=mesh, in_specs=in_specs, out_specs=P(ALL, None), check_vma=False
    )
```

```python
import functools
import math

import jax
import jax.numpy as jnp
from jax import lax
from jax.experimental import pallas as pl
from jax.experimental.pallas import tpu as pltpu
from jax.sharding import PartitionSpec as P

HEADS = 4
SUB = 8
LANES = 128
ALL = ("doc", "ctx")


def call(kernel, name, vmem=32, **options):
    return pl.pallas_call(
        kernel,
        name=name,
        compiler_params=pltpu.CompilerParams(vmem_limit_bytes=vmem * 1024 * 1024),
        **options,
    )


def scatter_pieces(stage, piece_index, values, blocks, capacity, piece):
    for slot in range(capacity):
        for lane in range(piece // LANES):
            stage[
                slot * (piece // LANES) + lane, pl.ds(piece_index, blocks, stride=SUB), :
            ] = values[slot * blocks : (slot + 1) * blocks, lane * LANES : (lane + 1) * LANES]


def gather_pieces(stage, piece_index, blocks, capacity, piece):
    return jnp.concatenate(
        [
            jnp.concatenate(
                [
                    stage[slot * (piece // LANES) + lane, pl.ds(piece_index, blocks, stride=SUB), :]
                    for lane in range(piece // LANES)
                ],
                axis=1,
            ).astype(jnp.bfloat16)
            for slot in range(capacity)
        ],
        axis=0,
    )


def fill_stage(stage, sources):
    start = 0
    for source in sources:
        for lane in range(source.shape[1] // LANES):
            stage[start] = source[:, lane * LANES : (lane + 1) * LANES].astype(jnp.float32)
            start += 1


def drain_stage(stage, targets):
    start = 0
    for target in targets:
        for lane in range(target.shape[1] // LANES):
            target[:, lane * LANES : (lane + 1) * LANES] = stage[start].astype(target.dtype)
            start += 1


def as_column(row):
    n = row.shape[1]
    on_diagonal = lax.broadcasted_iota(jnp.int32, (n, n), 0) == lax.broadcasted_iota(
        jnp.int32, (n, n), 1
    )
    return jnp.sum(jnp.where(on_diagonal, row, jnp.zeros_like(row)), axis=1, keepdims=True)


def as_row(column):
    n = column.shape[0]
    on_diagonal = lax.broadcasted_iota(jnp.int32, (n, n), 0) == lax.broadcasted_iota(
        jnp.int32, (n, n), 1
    )
    return jnp.sum(jnp.where(on_diagonal, column, jnp.zeros_like(column)), axis=0, keepdims=True)


def place_kernel(
    blocks, capacity, owner_row, module_row, doc_row, requests, first_sent, second_sent, tags, slots, stage
):
    rows, width = requests.shape
    piece = width // SUB
    modules = module_row[...]
    owners = as_column(owner_row[...])
    named = lax.broadcasted_iota(jnp.int32, (blocks, rows), 0) == modules
    target = jnp.sum(jnp.where(named, owners, 0), axis=0, keepdims=True)
    first = lax.broadcasted_iota(jnp.int32, (rows, rows), 0)
    second = lax.broadcasted_iota(jnp.int32, (rows, rows), 1)
    ahead = (as_column(modules) == modules) & (first < second)
    rank = jnp.sum(ahead.astype(jnp.int32), axis=0, keepdims=True)
    slot_row = rank * blocks + target
    slots[...] = slot_row
    slot_column = as_column(slot_row)
    documents = as_column(doc_row[...] + 1)
    for part in range(tags.shape[0]):
        lanes = lax.broadcasted_iota(jnp.int32, (rows, LANES), 1) + part * LANES
        tags[part : part + 1, :] = jnp.sum(
            jnp.where(lanes == slot_column, documents, 0), axis=0, keepdims=True
        ).astype(jnp.float32)
    slot_ids = lax.broadcasted_iota(jnp.int32, (capacity * blocks, rows), 0)
    placer = (slot_ids == slot_row).astype(jnp.float32).astype(jnp.bfloat16)
    for index in range(SUB):
        moved = jnp.dot(
            placer,
            requests[:, index * piece : (index + 1) * piece],
            preferred_element_type=jnp.float32,
        )
        scatter_pieces(stage, index, moved, blocks, capacity, piece)
    drain_stage(stage, (first_sent, second_sent))


def attend_kernel(
    chunks, tokens, w_keys, w_values, latents, tags, partial, tokens_in, keys_in, values_in, done
):
    depth = w_keys.shape[0] // chunks
    copies = []
    for chunk in range(chunks):
        part = pl.ds(chunk * depth, depth)
        copies.append(
            [
                pltpu.make_async_copy(
                    tokens.at[0, :, part], tokens_in.at[chunk], done.at[chunk, 0]
                ),
                pltpu.make_async_copy(w_keys.at[part, :], keys_in.at[chunk], done.at[chunk, 1]),
                pltpu.make_async_copy(w_values.at[part, :], values_in.at[chunk], done.at[chunk, 2]),
            ]
        )
    for group in copies:
        for copy in group:
            copy.start()
    keys = values = 0.0
    for chunk in range(chunks):
        for copy in copies[chunk]:
            copy.wait()
        keys = keys + jnp.dot(
            tokens_in[chunk], keys_in[chunk], preferred_element_type=jnp.float32
        )
        values = values + jnp.dot(
            tokens_in[chunk], values_in[chunk], preferred_element_type=jnp.float32
        )
    latent_count, width = latents.shape
    head_dim = width // HEADS
    queries = latents[...].astype(jnp.bfloat16)
    key_rows = keys.astype(jnp.bfloat16)
    value_rows = values.astype(jnp.bfloat16).astype(jnp.float32)
    peaks, sums = [], []
    for head in range(HEADS):
        lanes = slice(head * head_dim, (head + 1) * head_dim)
        scores = lax.dot_general(
            queries[:, lanes],
            key_rows[:, lanes],
            (((1,), (1,)), ((), ())),
            preferred_element_type=jnp.float32,
        ) / math.sqrt(head_dim)
        peak = jnp.max(scores, axis=1, keepdims=True)
        expo = jnp.exp(scores - peak)
        peaks.append(peak)
        sums.append(jnp.sum(expo, axis=1, keepdims=True))
        partial[head * latent_count : (head + 1) * latent_count, :] = jnp.dot(
            expo,
            value_rows[:, lanes],
            precision=lax.Precision.HIGHEST,
            preferred_element_type=jnp.float32,
        )
    entries = HEADS * latent_count
    partial[entries:, :] = jnp.zeros_like(partial[entries:, :])
    partial[entries : entries + 1, :entries] = as_row(jnp.concatenate(peaks, axis=0))
    partial[entries + 1 : entries + 2, :entries] = as_row(jnp.concatenate(sums, axis=0))
    partial[entries + 2 : entries + 2 + tags.shape[0], :] = tags[...]


def summary_kernel(tag_parts, pieces, latents, w_out, gain, packet):
    members = pieces.shape[0]
    latent_count, width = latents.shape
    entries = HEADS * latent_count
    peaks = [as_column(pieces[c, entries : entries + 1, :entries]) for c in range(members)]
    summit = functools.reduce(jnp.maximum, peaks)
    total, weighted = 0.0, 0.0
    for c in range(members):
        ratio = jnp.exp(peaks[c] - summit)
        total = total + as_column(pieces[c, entries + 1 : entries + 2, :entries]) * ratio
        weighted = weighted + pieces[c, :entries, :] * ratio
    attended = weighted / total
    attended = jnp.concatenate(
        [attended[h * latent_count : (h + 1) * latent_count] for h in range(HEADS)], axis=1
    ).astype(jnp.bfloat16)
    mixed = latents[...] + jnp.dot(attended, w_out[...], preferred_element_type=jnp.float32)
    summary = (
        mixed
        * lax.rsqrt(jnp.mean(mixed * mixed, axis=1, keepdims=True) + 1e-06)
        * gain[...]
    )
    packet[:latent_count, :] = summary.astype(jnp.bfloat16)
    tag_rows = [
        jnp.concatenate(
            [pieces[c, entries + 2 + part : entries + 3 + part, :] for part in range(tag_parts)],
            axis=1,
        )
        for c in range(members)
    ]
    block = jnp.concatenate(tag_rows, axis=0)
    block = jnp.pad(
        block,
        ((0, packet.shape[0] - latent_count - members), (0, width - tag_parts * LANES)),
    )
    packet[latent_count:, :] = block.astype(jnp.bfloat16)


def factor_kernel(
    blocks,
    capacity,
    early,
    latent_count,
    chunks,
    me,
    everyone,
    heads_down,
    heads_up,
    down,
    up,
    tags_first,
    tags_second,
    heads_in,
    factors_out,
    arrived,
    left,
):
    depth = down.shape[1] // chunks
    jobs = []
    for chunk in range(chunks):
        part = pl.ds(chunk * depth, depth)
        for side, (heads, factor) in enumerate(((heads_down, down), (heads_up, up))):
            jobs.append(
                (
                    chunk,
                    side,
                    pltpu.make_async_copy(
                        heads.at[0, :, part], heads_in.at[chunk, side], arrived.at[chunk, side]
                    ),
                    pltpu.make_async_copy(
                        factors_out.at[chunk, side], factor.at[:, part], left.at[chunk, side]
                    ),
                )
            )
    for job in jobs:
        job[2].start()
    documents = everyone.shape[0]
    members = blocks // documents
    summaries = jnp.concatenate([everyone[x, :latent_count, :] for x in range(documents)], axis=0)
    device = me[0, 0]
    my_doc = device // members
    by_entry = jnp.concatenate(
        [everyone[x, latent_count:, :].astype(jnp.float32)[:members] for x in range(documents)],
        axis=0,
    ).astype(jnp.bfloat16)
    source = lax.broadcasted_iota(jnp.int32, (blocks, blocks), 0)
    entry = lax.broadcasted_iota(jnp.int32, (blocks, blocks), 1)
    sorter = source == ((entry // members) ^ my_doc) * members + entry % members
    sorter = sorter.astype(jnp.float32).astype(jnp.bfloat16)
    arranged = jnp.dot(sorter, by_entry, preferred_element_type=jnp.float32)
    lanes = lax.broadcasted_iota(jnp.int32, arranged.shape, 1)
    for slot in range(capacity):
        column = jnp.sum(
            jnp.where(lanes == slot * blocks + device, arranged, 0.0), axis=1, keepdims=True
        ).astype(jnp.int32)
        target, position = (tags_first, slot) if slot < early else (tags_second, slot - early)
        target[position * blocks : (position + 1) * blocks, :] = column
    for chunk, side, arriving, leaving in jobs:
        arriving.wait()
        factors_out[chunk, side] = jnp.dot(
            summaries, heads_in[chunk, side], preferred_element_type=jnp.float32
        ).astype(jnp.bfloat16)
        leaving.start()
    for job in jobs:
        job[3].wait()


def apply_kernel(blocks, capacity, latent_count, members, me, tags, down, up, arrived, *refs):
    *ready, update, arrived_in, stage, done = refs
    width = down.shape[1]
    piece = width // SUB
    start = sum(part.shape[1] for part in ready)
    incoming = [
        pltpu.make_async_copy(
            arrived.at[:, pl.ds(slot * piece, piece)], arrived_in.at[slot], done.at[slot]
        )
        for slot in range(capacity)
    ] + [pltpu.make_async_copy(part, update.at[:, pl.ds(0, start)], done.at[capacity]) for part in ready]
    for copy in incoming:
        copy.start()
    for slot in range(capacity):
        incoming[slot].wait()
        for lane in range(piece // LANES):
            stage[slot * (piece // LANES) + lane] = arrived_in[
                slot, :, lane * LANES : (lane + 1) * LANES
            ].astype(jnp.float32)
    coeff = None
    for index in range(SUB):
        part = lax.dot_general(
            gather_pieces(stage, index, blocks, capacity, piece),
            down[:, index * piece : (index + 1) * piece],
            (((1,), (1,)), ((), ())),
            preferred_element_type=jnp.float32,
        )
        coeff = part if coeff is None else coeff + part
    column_doc = (
        lax.broadcasted_iota(jnp.int32, coeff.shape, 1) // latent_count
    ) ^ (me[0, 0] // members)
    matched = tags[...] - 1 == column_doc
    coeff = jnp.where(matched, coeff / math.sqrt(width), 0.0).astype(jnp.bfloat16)
    for index in range(SUB):
        moved = jnp.dot(
            coeff, up[:, index * piece : (index + 1) * piece], preferred_element_type=jnp.float32
        ) * (1.0 / math.sqrt(latent_count))
        scatter_pieces(stage, index, moved, blocks, capacity, piece)
    drain_stage(stage, (update.at[:, start:],))
    for copy in incoming[capacity:]:
        copy.wait()


def finish_kernel(blocks, capacity, returned, slots, requests, adapted, adapted_out, stage, done):
    rows, width = requests.shape
    piece = width // SUB
    fill_stage(stage, (returned,))
    placed = lax.broadcasted_iota(jnp.int32, (capacity * blocks, rows), 0) == slots[...]
    placer = placed.astype(jnp.float32).astype(jnp.bfloat16)
    leaving = []
    for index in range(SUB):
        gathered = lax.dot_general(
            placer,
            gather_pieces(stage, index, blocks, capacity, piece),
            (((0,), (0,)), ((), ())),
            preferred_element_type=jnp.float32,
        )
        adapted_out[index] = (
            requests[:, index * piece : (index + 1) * piece].astype(jnp.float32) + gathered
        ).astype(adapted.dtype)
        leaving.append(
            pltpu.make_async_copy(
                adapted_out.at[index], adapted.at[:, pl.ds(index * piece, piece)], done.at[index]
            )
        )
        leaving[index].start()
    for copy in leaving:
        copy.wait()


def on_device(
    tokens,
    latents,
    w_keys,
    w_values,
    w_out,
    latent_gain,
    heads_down,
    heads_up,
    owner,
    requests,
    req_doc,
    req_module,
):
    doc_count = lax.axis_size("doc")
    ctx_count = lax.axis_size("ctx")
    blocks = doc_count * ctx_count
    rows, width = requests.shape
    capacity = max(2, rows // blocks + 1)
    piece = width // SUB
    latent_count, latent_width = latents.shape
    head_dim = latent_width // HEADS
    my_doc = lax.axis_index("doc")
    my_ctx = lax.axis_index("ctx")
    early = max(1, (capacity - 1) // 2)
    late = capacity - early
    tag_parts = -(-(capacity * blocks) // LANES)
    me = (my_doc * ctx_count + my_ctx).astype(jnp.int32).reshape(1, 1)
    in_smem = pl.BlockSpec(memory_space=pltpu.SMEM)
    in_vmem = pl.BlockSpec(memory_space=pltpu.VMEM)
    in_hbm = pl.BlockSpec(memory_space=pl.ANY)
    outside = pl.BlockSpec(memory_space=pltpu.HBM)

    def after(values, *others):
        return lax.optimization_barrier((values, *others))[0]

    def block_type(slot_count):
        return jax.ShapeDtypeStruct((blocks * SUB, slot_count * piece), jnp.bfloat16)

    def stage_type(slot_count):
        return pltpu.VMEM((slot_count * piece // LANES, blocks * SUB, LANES), jnp.float32)

    def exchange(values):
        return lax.all_to_all(
            values.reshape(blocks, SUB, -1), ALL, split_axis=0, concat_axis=0, tiled=True
        ).reshape(values.shape)

    first_sent, second_sent, tags, slots = call(
        functools.partial(place_kernel, blocks, capacity),
        "place_rows",
        vmem=60,
        out_shape=(
            block_type(early),
            block_type(late),
            jax.ShapeDtypeStruct((tag_parts, LANES), jnp.float32),
            jax.ShapeDtypeStruct((1, rows), jnp.int32),
        ),
        scratch_shapes=[stage_type(capacity)],
    )(
        owner.reshape(1, blocks),
        req_module.reshape(1, rows),
        req_doc.reshape(1, rows),
        requests,
    )
    first_arrived = exchange(first_sent)

    token_count = tokens.shape[1]
    entries = HEADS * latent_count
    partial_rows = -(-(entries + 2 + tag_parts) // SUB) * SUB
    chunks = width // (SUB * LANES)
    depth = width // chunks
    partial = call(
        functools.partial(attend_kernel, chunks),
        "attend",
        vmem=60,
        in_specs=[in_hbm] * 3 + [in_vmem] * 2,
        out_shape=jax.ShapeDtypeStruct((partial_rows, head_dim), jnp.float32),
        scratch_shapes=[
            pltpu.VMEM((chunks, token_count, depth), jnp.bfloat16),
            pltpu.VMEM((chunks, depth, latent_width), jnp.bfloat16),
            pltpu.VMEM((chunks, depth, latent_width), jnp.bfloat16),
            pltpu.SemaphoreType.DMA((chunks, 3)),
        ],
    )(tokens, w_keys, w_values, latents, tags)
    packet_rows = latent_count + 16
    packet = call(
        functools.partial(summary_kernel, tag_parts),
        "summarize",
        out_shape=jax.ShapeDtypeStruct((packet_rows, latent_width), jnp.bfloat16),
    )(lax.all_gather(partial, "ctx"), latents, w_out, latent_gain.reshape(1, latent_width))

    share = doc_count // ctx_count
    fetched = []
    for turn in range(share):
        pairs = [
            (doc * ctx_count + ctx, (doc ^ (ctx * share + turn)) * ctx_count + ctx)
            for doc in range(doc_count)
            for ctx in range(ctx_count)
        ]
        fetched.append(lax.ppermute(packet, ALL, pairs))
    second_arrived = exchange(after(second_sent, *fetched))
    everyone = lax.all_gather(jnp.stack(fetched), "ctx").reshape(
        doc_count, packet_rows, latent_width
    )

    def tag_type(slot_count):
        return jax.ShapeDtypeStruct((slot_count * blocks, 1), jnp.int32)

    factor_type = jax.ShapeDtypeStruct((doc_count * latent_count, width), jnp.bfloat16)
    down_factor, up_factor, first_tags, second_tags = call(
        functools.partial(factor_kernel, blocks, capacity, early, latent_count, chunks),
        "factors",
        vmem=60,
        in_specs=[in_smem, in_vmem, in_hbm, in_hbm],
        out_specs=(in_hbm, in_hbm, in_vmem, in_vmem),
        out_shape=(factor_type, factor_type, tag_type(early), tag_type(late)),
        scratch_shapes=[
            pltpu.VMEM((chunks, 2, latent_width, depth), jnp.bfloat16),
            pltpu.VMEM((chunks, 2, doc_count * latent_count, depth), jnp.bfloat16),
            pltpu.SemaphoreType.DMA((chunks, 2)),
            pltpu.SemaphoreType.DMA((chunks, 2)),
        ],
    )(me, everyone, heads_down, heads_up)

    def apply(tag_column, slot_count, arrived, *ready):
        total = slot_count + sum(part.shape[1] for part in ready) // piece
        return call(
            functools.partial(apply_kernel, blocks, slot_count, latent_count, ctx_count),
            "apply_rows",
            in_specs=[in_smem] + [in_vmem] * 3 + [outside] * (1 + len(ready)),
            out_shape=block_type(total),
            scratch_shapes=[
                pltpu.VMEM((slot_count, blocks * SUB, piece), jnp.bfloat16),
                stage_type(slot_count),
                pltpu.SemaphoreType.DMA((slot_count + len(ready),)),
            ],
        )(me, tag_column, down_factor, up_factor, arrived, *ready)

    first_update = apply(first_tags, early, first_arrived)
    update = apply(second_tags, late, after(second_arrived, first_update), first_update)
    returned = exchange(update)
    return call(
        functools.partial(finish_kernel, blocks, capacity),
        "finish_rows",
        out_specs=outside,
        out_shape=jax.ShapeDtypeStruct((rows, width), jnp.bfloat16),
        scratch_shapes=[
            pltpu.VMEM((SUB, rows, piece), jnp.bfloat16),
            stage_type(capacity),
            pltpu.SemaphoreType.DMA((SUB,)),
        ],
    )(returned, slots, requests)


def solution(mesh):
    in_specs = (
        P("doc", "ctx", None),
        P(),
        P(),
        P(),
        P(),
        P(),
        P(ALL, None, None),
        P(ALL, None, None),
        P(),
        P(ALL, None),
        P(ALL),
        P(ALL, None),
    )
    return jax.shard_map(
        on_device, mesh=mesh, in_specs=in_specs, out_specs=P(ALL, None), check_vma=False
    )
```

```python
import functools
import math

import jax
import jax.numpy as jnp
from jax import lax
from jax.experimental import pallas as pl
from jax.experimental.pallas import tpu as pltpu
from jax.sharding import PartitionSpec as P

HEADS = 4
SUB = 8
LANES = 128
LONG = 20 * 1024 * 1024
ALL = ("doc", "ctx")


def call(kernel, name, vmem=32, **options):
    return pl.pallas_call(
        kernel,
        name=name,
        compiler_params=pltpu.CompilerParams(vmem_limit_bytes=vmem * 1024 * 1024),
        **options,
    )


def scatter_pieces(stage, piece_index, values, blocks, capacity, piece):
    for slot in range(capacity):
        for lane in range(piece // LANES):
            stage[
                slot * (piece // LANES) + lane, pl.ds(piece_index, blocks, stride=SUB), :
            ] = values[slot * blocks : (slot + 1) * blocks, lane * LANES : (lane + 1) * LANES]


def gather_pieces(stage, piece_index, blocks, capacity, piece):
    return jnp.concatenate(
        [
            jnp.concatenate(
                [
                    stage[slot * (piece // LANES) + lane, pl.ds(piece_index, blocks, stride=SUB), :]
                    for lane in range(piece // LANES)
                ],
                axis=1,
            ).astype(jnp.bfloat16)
            for slot in range(capacity)
        ],
        axis=0,
    )


def fill_stage(stage, sources):
    start = 0
    for source in sources:
        for lane in range(source.shape[1] // LANES):
            stage[start] = source[:, lane * LANES : (lane + 1) * LANES].astype(jnp.float32)
            start += 1


def drain_stage(stage, targets):
    start = 0
    for target in targets:
        for lane in range(target.shape[1] // LANES):
            target[:, lane * LANES : (lane + 1) * LANES] = stage[start].astype(target.dtype)
            start += 1


def as_column(row):
    n = row.shape[1]
    on_diagonal = lax.broadcasted_iota(jnp.int32, (n, n), 0) == lax.broadcasted_iota(
        jnp.int32, (n, n), 1
    )
    return jnp.sum(jnp.where(on_diagonal, row, jnp.zeros_like(row)), axis=1, keepdims=True)


def as_row(column):
    n = column.shape[0]
    on_diagonal = lax.broadcasted_iota(jnp.int32, (n, n), 0) == lax.broadcasted_iota(
        jnp.int32, (n, n), 1
    )
    return jnp.sum(jnp.where(on_diagonal, column, jnp.zeros_like(column)), axis=0, keepdims=True)


def place_kernel(
    blocks, capacity, owner_row, module_row, doc_row, requests, first_sent, second_sent, tags, slots, stage
):
    rows, width = requests.shape
    piece = width // SUB
    modules = module_row[...]
    owners = as_column(owner_row[...])
    named = lax.broadcasted_iota(jnp.int32, (blocks, rows), 0) == modules
    target = jnp.sum(jnp.where(named, owners, 0), axis=0, keepdims=True)
    first = lax.broadcasted_iota(jnp.int32, (rows, rows), 0)
    second = lax.broadcasted_iota(jnp.int32, (rows, rows), 1)
    ahead = (as_column(modules) == modules) & (first < second)
    rank = jnp.sum(ahead.astype(jnp.int32), axis=0, keepdims=True)
    slot_row = rank * blocks + target
    slots[...] = slot_row
    slot_column = as_column(slot_row)
    documents = as_column(doc_row[...] + 1)
    for part in range(tags.shape[0]):
        lanes = lax.broadcasted_iota(jnp.int32, (rows, LANES), 1) + part * LANES
        tags[part : part + 1, :] = jnp.sum(
            jnp.where(lanes == slot_column, documents, 0), axis=0, keepdims=True
        ).astype(jnp.float32)
    slot_ids = lax.broadcasted_iota(jnp.int32, (capacity * blocks, rows), 0)
    placer = (slot_ids == slot_row).astype(jnp.float32).astype(jnp.bfloat16)
    for index in range(SUB):
        moved = jnp.dot(
            placer,
            requests[:, index * piece : (index + 1) * piece],
            preferred_element_type=jnp.float32,
        )
        scatter_pieces(stage, index, moved, blocks, capacity, piece)
    drain_stage(stage, (first_sent, second_sent))


def attend_kernel(
    chunks, tokens, w_keys, w_values, latents, tags, partial, tokens_in, keys_in, values_in, done
):
    depth = w_keys.shape[0] // chunks
    copies = []
    for chunk in range(chunks):
        part = pl.ds(chunk * depth, depth)
        copies.append(
            [
                pltpu.make_async_copy(
                    tokens.at[0, :, part], tokens_in.at[chunk], done.at[chunk, 0]
                ),
                pltpu.make_async_copy(w_keys.at[part, :], keys_in.at[chunk], done.at[chunk, 1]),
                pltpu.make_async_copy(w_values.at[part, :], values_in.at[chunk], done.at[chunk, 2]),
            ]
        )
    for group in copies:
        for copy in group:
            copy.start()
    keys = values = 0.0
    for chunk in range(chunks):
        for copy in copies[chunk]:
            copy.wait()
        keys = keys + jnp.dot(
            tokens_in[chunk], keys_in[chunk], preferred_element_type=jnp.float32
        )
        values = values + jnp.dot(
            tokens_in[chunk], values_in[chunk], preferred_element_type=jnp.float32
        )
    latent_count, width = latents.shape
    head_dim = width // HEADS
    queries = latents[...].astype(jnp.bfloat16)
    key_rows = keys.astype(jnp.bfloat16)
    value_rows = values.astype(jnp.bfloat16).astype(jnp.float32)
    peaks, sums = [], []
    for head in range(HEADS):
        lanes = slice(head * head_dim, (head + 1) * head_dim)
        scores = lax.dot_general(
            queries[:, lanes],
            key_rows[:, lanes],
            (((1,), (1,)), ((), ())),
            preferred_element_type=jnp.float32,
        ) / math.sqrt(head_dim)
        peak = jnp.max(scores, axis=1, keepdims=True)
        expo = jnp.exp(scores - peak)
        peaks.append(peak)
        sums.append(jnp.sum(expo, axis=1, keepdims=True))
        partial[head * latent_count : (head + 1) * latent_count, :] = jnp.dot(
            expo,
            value_rows[:, lanes],
            precision=lax.Precision.HIGHEST,
            preferred_element_type=jnp.float32,
        )
    entries = HEADS * latent_count
    partial[entries:, :] = jnp.zeros_like(partial[entries:, :])
    partial[entries : entries + 1, :entries] = as_row(jnp.concatenate(peaks, axis=0))
    partial[entries + 1 : entries + 2, :entries] = as_row(jnp.concatenate(sums, axis=0))
    partial[entries + 2 : entries + 2 + tags.shape[0], :] = tags[...]


def summary_kernel(tag_parts, pieces, latents, w_out, gain, packet):
    members = pieces.shape[0]
    latent_count, width = latents.shape
    entries = HEADS * latent_count
    peaks = [as_column(pieces[c, entries : entries + 1, :entries]) for c in range(members)]
    summit = functools.reduce(jnp.maximum, peaks)
    total, weighted = 0.0, 0.0
    for c in range(members):
        ratio = jnp.exp(peaks[c] - summit)
        total = total + as_column(pieces[c, entries + 1 : entries + 2, :entries]) * ratio
        weighted = weighted + pieces[c, :entries, :] * ratio
    attended = weighted / total
    attended = jnp.concatenate(
        [attended[h * latent_count : (h + 1) * latent_count] for h in range(HEADS)], axis=1
    ).astype(jnp.bfloat16)
    mixed = latents[...] + jnp.dot(attended, w_out[...], preferred_element_type=jnp.float32)
    summary = (
        mixed
        * lax.rsqrt(jnp.mean(mixed * mixed, axis=1, keepdims=True) + 1e-06)
        * gain[...]
    )
    packet[:latent_count, :] = summary.astype(jnp.bfloat16)
    tag_rows = [
        jnp.concatenate(
            [pieces[c, entries + 2 + part : entries + 3 + part, :] for part in range(tag_parts)],
            axis=1,
        )
        for c in range(members)
    ]
    block = jnp.concatenate(tag_rows, axis=0)
    block = jnp.pad(
        block,
        ((0, packet.shape[0] - latent_count - members), (0, width - tag_parts * LANES)),
    )
    packet[latent_count:, :] = block.astype(jnp.bfloat16)


def factor_kernel(
    blocks,
    capacity,
    early,
    latent_count,
    chunks,
    me,
    everyone,
    heads_down,
    heads_up,
    down,
    up,
    tags_first,
    tags_second,
    heads_in,
    factors_out,
    arrived,
    left,
):
    depth = down.shape[1] // chunks
    jobs = []
    for chunk in range(chunks):
        part = pl.ds(chunk * depth, depth)
        for side, (heads, factor) in enumerate(((heads_down, down), (heads_up, up))):
            jobs.append(
                (
                    chunk,
                    side,
                    pltpu.make_async_copy(
                        heads.at[0, :, part], heads_in.at[chunk, side], arrived.at[chunk, side]
                    ),
                    pltpu.make_async_copy(
                        factors_out.at[chunk, side], factor.at[:, part], left.at[chunk, side]
                    ),
                )
            )
    for job in jobs:
        job[2].start()
    documents = everyone.shape[0]
    members = blocks // documents
    summaries = jnp.concatenate([everyone[x, :latent_count, :] for x in range(documents)], axis=0)
    device = me[0, 0]
    my_doc = device // members
    by_entry = jnp.concatenate(
        [
            everyone[x, latent_count : latent_count + members, :].astype(jnp.float32)
            for x in range(documents)
        ],
        axis=0,
    ).astype(jnp.bfloat16)
    source = lax.broadcasted_iota(jnp.int32, (blocks, blocks), 0)
    entry = lax.broadcasted_iota(jnp.int32, (blocks, blocks), 1)
    sorter = source == ((entry // members) ^ my_doc) * members + entry % members
    sorter = sorter.astype(jnp.float32).astype(jnp.bfloat16)
    arranged = jnp.dot(sorter, by_entry, preferred_element_type=jnp.float32)
    lanes = lax.broadcasted_iota(jnp.int32, arranged.shape, 1)
    for slot in range(capacity):
        column = jnp.sum(
            jnp.where(lanes == slot * blocks + device, arranged, 0.0), axis=1, keepdims=True
        ).astype(jnp.int32)
        target, position = (tags_first, slot) if slot < early else (tags_second, slot - early)
        target[position * blocks : (position + 1) * blocks, :] = column
    for chunk, side, arriving, leaving in jobs:
        arriving.wait()
        factors_out[chunk, side] = jnp.dot(
            summaries, heads_in[chunk, side], preferred_element_type=jnp.float32
        ).astype(jnp.bfloat16)
        leaving.start()
    for job in jobs:
        job[3].wait()


def coeff_kernel(blocks, capacity, latent_count, members, me, tags, down, arrived, *refs):
    coeff_out, arrived_in, stage, done = refs
    coeff_out[...] = coefficients(
        blocks, capacity, latent_count, members, me, tags, down, arrived, arrived_in, stage, done
    )


def coefficients(
    blocks, capacity, latent_count, members, me, tags, down, arrived, arrived_in, stage, done, *later
):
    width = down.shape[1]
    piece = width // SUB
    incoming = [
        pltpu.make_async_copy(
            arrived.at[:, pl.ds(slot * piece, piece)], arrived_in.at[slot], done.at[slot]
        )
        for slot in range(capacity)
    ]
    for copy in incoming + list(later):
        copy.start()
    for slot in range(capacity):
        incoming[slot].wait()
        for lane in range(piece // LANES):
            stage[slot * (piece // LANES) + lane] = arrived_in[
                slot, :, lane * LANES : (lane + 1) * LANES
            ].astype(jnp.float32)
    coeff = 0.0
    for index in range(SUB):
        coeff = coeff + lax.dot_general(
            gather_pieces(stage, index, blocks, capacity, piece),
            down[:, index * piece : (index + 1) * piece],
            (((1,), (1,)), ((), ())),
            preferred_element_type=jnp.float32,
        )
    column_doc = (
        lax.broadcasted_iota(jnp.int32, coeff.shape, 1) // latent_count
    ) ^ (me[0, 0] // members)
    matched = tags[...] - 1 == column_doc
    return jnp.where(matched, coeff / math.sqrt(width), 0.0).astype(jnp.bfloat16)


def update_kernel(
    blocks, capacity, latent_count, members, me, tags, down, up, first_coeff, arrived, *refs
):
    update, arrived_in, stage, done, up_in, up_done = refs
    piece = down.shape[1] // SUB
    late = arrived.shape[1] // piece
    up_copy = pltpu.make_async_copy(up.at[:, pl.ds(0, down.shape[1])], up_in, up_done)
    coeff = coefficients(
        blocks, late, latent_count, members, me, tags, down, arrived, arrived_in, stage, done, up_copy
    )
    coeff = jnp.concatenate([first_coeff[...], coeff], axis=0)
    up_copy.wait()
    for index in range(SUB):
        moved = jnp.dot(
            coeff, up_in[:, index * piece : (index + 1) * piece], preferred_element_type=jnp.float32
        ) * (1.0 / math.sqrt(latent_count))
        scatter_pieces(stage, index, moved, blocks, capacity, piece)
    drain_stage(stage, (update,))


def finish_kernel(blocks, capacity, returned, slots, requests, adapted, adapted_out, stage, done):
    rows, width = requests.shape
    piece = width // SUB
    fill_stage(stage, (returned,))
    placed = lax.broadcasted_iota(jnp.int32, (capacity * blocks, rows), 0) == slots[...]
    placer = placed.astype(jnp.float32).astype(jnp.bfloat16)
    leaving = []
    for index in range(SUB):
        gathered = lax.dot_general(
            placer,
            gather_pieces(stage, index, blocks, capacity, piece),
            (((0,), (0,)), ((), ())),
            preferred_element_type=jnp.float32,
        )
        adapted_out[index] = (
            requests[:, index * piece : (index + 1) * piece].astype(jnp.float32) + gathered
        ).astype(adapted.dtype)
        leaving.append(
            pltpu.make_async_copy(
                adapted_out.at[index], adapted.at[:, pl.ds(index * piece, piece)], done.at[index]
            )
        )
        leaving[index].start()
    for copy in leaving:
        copy.wait()


def on_device(
    tokens,
    latents,
    w_keys,
    w_values,
    w_out,
    latent_gain,
    heads_down,
    heads_up,
    owner,
    requests,
    req_doc,
    req_module,
):
    doc_count = lax.axis_size("doc")
    ctx_count = lax.axis_size("ctx")
    blocks = doc_count * ctx_count
    rows, width = requests.shape
    capacity = max(2, rows // blocks + 1)
    piece = width // SUB
    latent_count, latent_width = latents.shape
    head_dim = latent_width // HEADS
    my_doc = lax.axis_index("doc")
    my_ctx = lax.axis_index("ctx")
    early = max(1, (capacity - 1) // 2)
    late = capacity - early
    tag_parts = -(-(capacity * blocks) // LANES)
    me = (my_doc * ctx_count + my_ctx).astype(jnp.int32).reshape(1, 1)
    in_smem = pl.BlockSpec(memory_space=pltpu.SMEM)
    in_vmem = pl.BlockSpec(memory_space=pltpu.VMEM)
    in_hbm = pl.BlockSpec(memory_space=pl.ANY)
    outside = pl.BlockSpec(memory_space=pltpu.HBM)

    def after(values, *others):
        return lax.optimization_barrier((values, *others))[0]

    def block_type(slot_count):
        return jax.ShapeDtypeStruct((blocks * SUB, slot_count * piece), jnp.bfloat16)

    def stage_type(slot_count):
        return pltpu.VMEM((slot_count * piece // LANES, blocks * SUB, LANES), jnp.float32)

    def exchange(values):
        return lax.all_to_all(
            values.reshape(blocks, SUB, -1), ALL, split_axis=0, concat_axis=0, tiled=True
        ).reshape(values.shape)

    first_sent, second_sent, tags, slots = call(
        functools.partial(place_kernel, blocks, capacity),
        "place_rows",
        vmem=60,
        out_shape=(
            block_type(early),
            block_type(late),
            jax.ShapeDtypeStruct((tag_parts, LANES), jnp.float32),
            jax.ShapeDtypeStruct((1, rows), jnp.int32),
        ),
        scratch_shapes=[stage_type(capacity)],
    )(
        owner.reshape(1, blocks),
        req_module.reshape(1, rows),
        req_doc.reshape(1, rows),
        requests,
    )
    first_arrived = exchange(first_sent)

    token_count = tokens.shape[1]
    entries = HEADS * latent_count
    partial_rows = -(-(entries + 2 + tag_parts) // SUB) * SUB
    chunks = width // (SUB * LANES)
    depth = width // chunks
    partial = call(
        functools.partial(attend_kernel, chunks),
        "attend",
        vmem=60,
        in_specs=[in_hbm] * 3 + [in_vmem] * 2,
        out_shape=jax.ShapeDtypeStruct((partial_rows, head_dim), jnp.float32),
        scratch_shapes=[
            pltpu.VMEM((chunks, token_count, depth), jnp.bfloat16),
            pltpu.VMEM((chunks, depth, latent_width), jnp.bfloat16),
            pltpu.VMEM((chunks, depth, latent_width), jnp.bfloat16),
            pltpu.SemaphoreType.DMA((chunks, 3)),
        ],
    )(tokens, w_keys, w_values, latents, tags)
    packet_rows = latent_count + -(-ctx_count // SUB) * SUB
    packet = call(
        functools.partial(summary_kernel, tag_parts),
        "summarize",
        out_shape=jax.ShapeDtypeStruct((packet_rows, latent_width), jnp.bfloat16),
    )(lax.all_gather(partial, "ctx"), latents, w_out, latent_gain.reshape(1, latent_width))

    share = doc_count // ctx_count
    fetched = []
    for turn in range(share):
        pairs = [
            (doc * ctx_count + ctx, (doc ^ (ctx * share + turn)) * ctx_count + ctx)
            for doc in range(doc_count)
            for ctx in range(ctx_count)
        ]
        fetched.append(lax.ppermute(packet, ALL, pairs))
    second_arrived = exchange(after(second_sent, *fetched))
    everyone = lax.all_gather(jnp.stack(fetched), "ctx").reshape(
        doc_count, packet_rows, latent_width
    )

    def tag_type(slot_count):
        return jax.ShapeDtypeStruct((slot_count * blocks, 1), jnp.int32)

    factor_type = jax.ShapeDtypeStruct((doc_count * latent_count, width), jnp.bfloat16)
    long_columns = -(-LONG // (doc_count * latent_count) // LANES) * LANES
    long_type = jax.ShapeDtypeStruct(
        (doc_count * latent_count, max(width, long_columns)), jnp.bfloat16
    )
    down_factor, up_factor, first_tags, second_tags = call(
        functools.partial(factor_kernel, blocks, capacity, early, latent_count, chunks),
        "factors",
        vmem=60,
        in_specs=[in_smem, in_vmem, in_hbm, in_hbm],
        out_specs=(in_hbm, in_hbm, in_vmem, in_vmem),
        out_shape=(factor_type, long_type, tag_type(early), tag_type(late)),
        scratch_shapes=[
            pltpu.VMEM((chunks, 2, latent_width, depth), jnp.bfloat16),
            pltpu.VMEM((chunks, 2, doc_count * latent_count, depth), jnp.bfloat16),
            pltpu.SemaphoreType.DMA((chunks, 2)),
            pltpu.SemaphoreType.DMA((chunks, 2)),
        ],
    )(me, everyone, heads_down, heads_up)

    def row_scratch(slot_count, stage_count):
        return [
            pltpu.VMEM((slot_count, blocks * SUB, piece), jnp.bfloat16),
            stage_type(stage_count),
            pltpu.SemaphoreType.DMA((slot_count,)),
        ]

    first_coeff = call(
        functools.partial(coeff_kernel, blocks, early, latent_count, ctx_count),
        "coefficients",
        in_specs=[in_smem] + [in_vmem] * 2 + [outside],
        out_shape=jax.ShapeDtypeStruct(
            (early * blocks, doc_count * latent_count), jnp.bfloat16
        ),
        scratch_shapes=row_scratch(early, early),
    )(me, first_tags, down_factor, first_arrived)
    update = call(
        functools.partial(update_kernel, blocks, capacity, latent_count, ctx_count),
        "update",
        in_specs=[in_smem] + [in_vmem] * 2 + [outside, in_vmem, outside],
        out_shape=block_type(capacity),
        scratch_shapes=row_scratch(late, capacity)
        + [pltpu.VMEM(factor_type.shape, factor_type.dtype), pltpu.SemaphoreType.DMA],
    )(me, second_tags, down_factor, up_factor, first_coeff, second_arrived)
    returned = exchange(update)
    return call(
        functools.partial(finish_kernel, blocks, capacity),
        "finish_rows",
        out_specs=outside,
        out_shape=jax.ShapeDtypeStruct((rows, width), jnp.bfloat16),
        scratch_shapes=[
            pltpu.VMEM((SUB, rows, piece), jnp.bfloat16),
            stage_type(capacity),
            pltpu.SemaphoreType.DMA((SUB,)),
        ],
    )(returned, slots, requests)


def solution(mesh):
    in_specs = (
        P("doc", "ctx", None),
        P(),
        P(),
        P(),
        P(),
        P(),
        P(ALL, None, None),
        P(ALL, None, None),
        P(),
        P(ALL, None),
        P(ALL),
        P(ALL, None),
    )
    return jax.shard_map(
        on_device, mesh=mesh, in_specs=in_specs, out_specs=P(ALL, None), check_vma=False
    )
```

```python
import functools
import math

import jax
import jax.numpy as jnp
from jax import lax
from jax.experimental import pallas as pl
from jax.experimental.pallas import tpu as pltpu
from jax.sharding import PartitionSpec as P

HEADS = 4
SUB = 8
LANES = 128
LONG = 20 * 1024 * 1024
ALL = ("doc", "ctx")


def call(kernel, name, vmem=32, **options):
    return pl.pallas_call(
        kernel,
        name=name,
        compiler_params=pltpu.CompilerParams(vmem_limit_bytes=vmem * 1024 * 1024),
        **options,
    )


def scatter_pieces(stage, piece_index, values, blocks, capacity, piece):
    for slot in range(capacity):
        for lane in range(piece // LANES):
            stage[
                slot * (piece // LANES) + lane, pl.ds(piece_index, blocks, stride=SUB), :
            ] = values[slot * blocks : (slot + 1) * blocks, lane * LANES : (lane + 1) * LANES]


def gather_pieces(stage, piece_index, blocks, capacity, piece):
    return jnp.concatenate(
        [
            jnp.concatenate(
                [
                    stage[slot * (piece // LANES) + lane, pl.ds(piece_index, blocks, stride=SUB), :]
                    for lane in range(piece // LANES)
                ],
                axis=1,
            ).astype(jnp.bfloat16)
            for slot in range(capacity)
        ],
        axis=0,
    )


def fill_stage(stage, sources):
    start = 0
    for source in sources:
        for lane in range(source.shape[1] // LANES):
            stage[start] = source[:, lane * LANES : (lane + 1) * LANES].astype(jnp.float32)
            start += 1


def drain_stage(stage, targets):
    start = 0
    for target in targets:
        for lane in range(target.shape[1] // LANES):
            target[:, lane * LANES : (lane + 1) * LANES] = stage[start].astype(target.dtype)
            start += 1


def as_column(row):
    n = row.shape[1]
    on_diagonal = lax.broadcasted_iota(jnp.int32, (n, n), 0) == lax.broadcasted_iota(
        jnp.int32, (n, n), 1
    )
    return jnp.sum(jnp.where(on_diagonal, row, jnp.zeros_like(row)), axis=1, keepdims=True)


def as_row(column):
    n = column.shape[0]
    on_diagonal = lax.broadcasted_iota(jnp.int32, (n, n), 0) == lax.broadcasted_iota(
        jnp.int32, (n, n), 1
    )
    return jnp.sum(jnp.where(on_diagonal, column, jnp.zeros_like(column)), axis=0, keepdims=True)


def place_kernel(
    blocks, capacity, owner_row, module_row, doc_row, requests, first_sent, second_sent, tags, slots, stage
):
    rows, width = requests.shape
    piece = width // SUB
    modules = module_row[...]
    owners = as_column(owner_row[...])
    named = lax.broadcasted_iota(jnp.int32, (blocks, rows), 0) == modules
    target = jnp.sum(jnp.where(named, owners, 0), axis=0, keepdims=True)
    first = lax.broadcasted_iota(jnp.int32, (rows, rows), 0)
    second = lax.broadcasted_iota(jnp.int32, (rows, rows), 1)
    ahead = (as_column(modules) == modules) & (first < second)
    rank = jnp.sum(ahead.astype(jnp.int32), axis=0, keepdims=True)
    slot_row = rank * blocks + target
    slots[...] = slot_row
    slot_column = as_column(slot_row)
    documents = as_column(doc_row[...] + 1)
    for part in range(tags.shape[0]):
        lanes = lax.broadcasted_iota(jnp.int32, (rows, LANES), 1) + part * LANES
        tags[part : part + 1, :] = jnp.sum(
            jnp.where(lanes == slot_column, documents, 0), axis=0, keepdims=True
        ).astype(jnp.float32)
    slot_ids = lax.broadcasted_iota(jnp.int32, (capacity * blocks, rows), 0)
    placer = (slot_ids == slot_row).astype(jnp.float32).astype(jnp.bfloat16)
    for index in range(SUB):
        moved = jnp.dot(
            placer,
            requests[:, index * piece : (index + 1) * piece],
            preferred_element_type=jnp.float32,
        )
        scatter_pieces(stage, index, moved, blocks, capacity, piece)
    drain_stage(stage, (first_sent, second_sent))


def attend_kernel(
    chunks, tokens, w_keys, w_values, latents, tags, partial, tokens_in, keys_in, values_in, done
):
    depth = w_keys.shape[0] // chunks
    copies = []
    for chunk in range(chunks):
        part = pl.ds(chunk * depth, depth)
        copies.append(
            [
                pltpu.make_async_copy(
                    tokens.at[0, :, part], tokens_in.at[chunk], done.at[chunk, 0]
                ),
                pltpu.make_async_copy(w_keys.at[part, :], keys_in.at[chunk], done.at[chunk, 1]),
                pltpu.make_async_copy(w_values.at[part, :], values_in.at[chunk], done.at[chunk, 2]),
            ]
        )
    for group in copies:
        for copy in group:
            copy.start()
    keys = values = 0.0
    for chunk in range(chunks):
        for copy in copies[chunk]:
            copy.wait()
        keys = keys + jnp.dot(
            tokens_in[chunk], keys_in[chunk], preferred_element_type=jnp.float32
        )
        values = values + jnp.dot(
            tokens_in[chunk], values_in[chunk], preferred_element_type=jnp.float32
        )
    latent_count, width = latents.shape
    head_dim = width // HEADS
    queries = latents[...].astype(jnp.bfloat16)
    key_rows = keys.astype(jnp.bfloat16)
    value_rows = values.astype(jnp.bfloat16).astype(jnp.float32)
    peaks, sums = [], []
    for head in range(HEADS):
        lanes = slice(head * head_dim, (head + 1) * head_dim)
        scores = lax.dot_general(
            queries[:, lanes],
            key_rows[:, lanes],
            (((1,), (1,)), ((), ())),
            preferred_element_type=jnp.float32,
        ) / math.sqrt(head_dim)
        peak = jnp.max(scores, axis=1, keepdims=True)
        expo = jnp.exp(scores - peak)
        peaks.append(peak)
        sums.append(jnp.sum(expo, axis=1, keepdims=True))
        partial[head * latent_count : (head + 1) * latent_count, :] = jnp.dot(
            expo,
            value_rows[:, lanes],
            precision=lax.Precision.HIGHEST,
            preferred_element_type=jnp.float32,
        )
    entries = HEADS * latent_count
    partial[entries:, :] = jnp.zeros_like(partial[entries:, :])
    partial[entries : entries + 1, :entries] = as_row(jnp.concatenate(peaks, axis=0))
    partial[entries + 1 : entries + 2, :entries] = as_row(jnp.concatenate(sums, axis=0))
    partial[entries + 2 : entries + 2 + tags.shape[0], :] = tags[...]


def summary_kernel(tag_parts, pieces, latents, w_out, gain, packet):
    members = pieces.shape[0]
    latent_count, width = latents.shape
    entries = HEADS * latent_count
    peaks = [as_column(pieces[c, entries : entries + 1, :entries]) for c in range(members)]
    summit = functools.reduce(jnp.maximum, peaks)
    total, weighted = 0.0, 0.0
    for c in range(members):
        ratio = jnp.exp(peaks[c] - summit)
        total = total + as_column(pieces[c, entries + 1 : entries + 2, :entries]) * ratio
        weighted = weighted + pieces[c, :entries, :] * ratio
    attended = weighted / total
    attended = jnp.concatenate(
        [attended[h * latent_count : (h + 1) * latent_count] for h in range(HEADS)], axis=1
    ).astype(jnp.bfloat16)
    mixed = latents[...] + jnp.dot(attended, w_out[...], preferred_element_type=jnp.float32)
    summary = (
        mixed
        * lax.rsqrt(jnp.mean(mixed * mixed, axis=1, keepdims=True) + 1e-06)
        * gain[...]
    )
    packet[:latent_count, :] = summary.astype(jnp.bfloat16)
    tag_rows = [
        jnp.concatenate(
            [pieces[c, entries + 2 + part : entries + 3 + part, :] for part in range(tag_parts)],
            axis=1,
        )
        for c in range(members)
    ]
    block = jnp.concatenate(tag_rows, axis=0)
    block = jnp.pad(
        block,
        ((0, packet.shape[0] - latent_count - members), (0, width - tag_parts * LANES)),
    )
    packet[latent_count:, :] = block.astype(jnp.bfloat16)


def factor_kernel(
    blocks,
    capacity,
    early,
    latent_count,
    chunks,
    me,
    everyone,
    heads_down,
    heads_up,
    down,
    up,
    tags_first,
    tags_second,
    heads_in,
    factors_out,
    arrived,
    left,
):
    depth = down.shape[1] // chunks
    jobs = []
    for chunk in range(chunks):
        part = pl.ds(chunk * depth, depth)
        for side, (heads, factor) in enumerate(((heads_down, down), (heads_up, up))):
            jobs.append(
                (
                    chunk,
                    side,
                    pltpu.make_async_copy(
                        heads.at[0, :, part], heads_in.at[chunk, side], arrived.at[chunk, side]
                    ),
                    pltpu.make_async_copy(
                        factors_out.at[chunk, side], factor.at[:, part], left.at[chunk, side]
                    ),
                )
            )
    for job in jobs:
        job[2].start()
    documents = everyone.shape[0]
    members = blocks // documents
    summaries = jnp.concatenate([everyone[x, :latent_count, :] for x in range(documents)], axis=0)
    device = me[0, 0]
    my_doc = device // members
    by_entry = jnp.concatenate(
        [
            everyone[x, latent_count : latent_count + members, :].astype(jnp.float32)
            for x in range(documents)
        ],
        axis=0,
    ).astype(jnp.bfloat16)
    source = lax.broadcasted_iota(jnp.int32, (blocks, blocks), 0)
    entry = lax.broadcasted_iota(jnp.int32, (blocks, blocks), 1)
    sorter = source == ((entry // members) ^ my_doc) * members + entry % members
    sorter = sorter.astype(jnp.float32).astype(jnp.bfloat16)
    arranged = jnp.dot(sorter, by_entry, preferred_element_type=jnp.float32)
    lanes = lax.broadcasted_iota(jnp.int32, arranged.shape, 1)
    for slot in range(capacity):
        column = jnp.sum(
            jnp.where(lanes == slot * blocks + device, arranged, 0.0), axis=1, keepdims=True
        ).astype(jnp.int32)
        target, position = (tags_first, slot) if slot < early else (tags_second, slot - early)
        target[position * blocks : (position + 1) * blocks, :] = column
    for chunk, side, arriving, leaving in jobs:
        arriving.wait()
        factors_out[chunk, side] = jnp.dot(
            summaries, heads_in[chunk, side], preferred_element_type=jnp.float32
        ).astype(jnp.bfloat16)
        leaving.start()
    for job in jobs:
        job[3].wait()


def coeff_kernel(blocks, capacity, latent_count, members, me, tags, down, arrived, *refs):
    coeff_out, stage = refs
    coeff_out[...] = coefficients(
        blocks, capacity, latent_count, members, me, tags, down, arrived, stage
    )


def coefficients(
    blocks, capacity, latent_count, members, me, tags, down, arrived, stage
):
    width = down.shape[1]
    piece = width // SUB
    for lane in range(capacity * piece // LANES):
        stage[lane] = arrived[:, lane * LANES : (lane + 1) * LANES].astype(jnp.float32)
    coeff = 0.0
    for index in range(SUB):
        coeff = coeff + lax.dot_general(
            gather_pieces(stage, index, blocks, capacity, piece),
            down[:, index * piece : (index + 1) * piece],
            (((1,), (1,)), ((), ())),
            preferred_element_type=jnp.float32,
        )
    column_doc = (
        lax.broadcasted_iota(jnp.int32, coeff.shape, 1) // latent_count
    ) ^ (me[0, 0] // members)
    matched = tags[...] - 1 == column_doc
    return jnp.where(matched, coeff / math.sqrt(width), 0.0).astype(jnp.bfloat16)


def update_kernel(
    blocks, capacity, latent_count, members, me, tags, down, up, first_coeff, arrived, *refs
):
    update, stage, up_in, up_done = refs
    piece = down.shape[1] // SUB
    late = arrived.shape[1] // piece
    up_copy = pltpu.make_async_copy(up.at[:, pl.ds(0, down.shape[1])], up_in, up_done)
    up_copy.start()
    coeff = coefficients(
        blocks, late, latent_count, members, me, tags, down, arrived, stage
    )
    coeff = jnp.concatenate([first_coeff[...], coeff], axis=0)
    up_copy.wait()
    for index in range(SUB):
        moved = jnp.dot(
            coeff, up_in[:, index * piece : (index + 1) * piece], preferred_element_type=jnp.float32
        ) * (1.0 / math.sqrt(latent_count))
        scatter_pieces(stage, index, moved, blocks, capacity, piece)
    drain_stage(stage, (update,))


def finish_kernel(blocks, capacity, returned, slots, requests, adapted, adapted_out, stage, done):
    rows, width = requests.shape
    piece = width // SUB
    fill_stage(stage, (returned,))
    slot_column = as_column(slots[...])
    wanted = lax.broadcasted_iota(jnp.int32, (rows, capacity * blocks), 1) == slot_column
    picker = wanted.astype(jnp.float32).astype(jnp.bfloat16)
    leaving = []
    for index in range(SUB):
        gathered = jnp.dot(
            picker,
            gather_pieces(stage, index, blocks, capacity, piece),
            preferred_element_type=jnp.float32,
        )
        adapted_out[index] = (
            requests[:, index * piece : (index + 1) * piece].astype(jnp.float32) + gathered
        ).astype(adapted.dtype)
        leaving.append(
            pltpu.make_async_copy(
                adapted_out.at[index], adapted.at[:, pl.ds(index * piece, piece)], done.at[index]
            )
        )
        leaving[index].start()
    for copy in leaving:
        copy.wait()


def on_device(
    tokens,
    latents,
    w_keys,
    w_values,
    w_out,
    latent_gain,
    heads_down,
    heads_up,
    owner,
    requests,
    req_doc,
    req_module,
):
    doc_count = lax.axis_size("doc")
    ctx_count = lax.axis_size("ctx")
    blocks = doc_count * ctx_count
    rows, width = requests.shape
    capacity = max(2, rows // blocks + 1)
    piece = width // SUB
    latent_count, latent_width = latents.shape
    head_dim = latent_width // HEADS
    my_doc = lax.axis_index("doc")
    my_ctx = lax.axis_index("ctx")
    early = max(1, (capacity - 1) // 2)
    late = capacity - early
    tag_parts = -(-(capacity * blocks) // LANES)
    me = (my_doc * ctx_count + my_ctx).astype(jnp.int32).reshape(1, 1)
    in_smem = pl.BlockSpec(memory_space=pltpu.SMEM)
    in_vmem = pl.BlockSpec(memory_space=pltpu.VMEM)
    in_hbm = pl.BlockSpec(memory_space=pl.ANY)
    outside = pl.BlockSpec(memory_space=pltpu.HBM)

    def after(values, *others):
        return lax.optimization_barrier((values, *others))[0]

    def block_type(slot_count):
        return jax.ShapeDtypeStruct((blocks * SUB, slot_count * piece), jnp.bfloat16)

    def stage_type(slot_count):
        return pltpu.VMEM((slot_count * piece // LANES, blocks * SUB, LANES), jnp.float32)

    def exchange(values):
        return lax.all_to_all(
            values.reshape(blocks, SUB, -1), ALL, split_axis=0, concat_axis=0, tiled=True
        ).reshape(values.shape)

    first_sent, second_sent, tags, slots = call(
        functools.partial(place_kernel, blocks, capacity),
        "place_rows",
        vmem=60,
        out_shape=(
            block_type(early),
            block_type(late),
            jax.ShapeDtypeStruct((tag_parts, LANES), jnp.float32),
            jax.ShapeDtypeStruct((1, rows), jnp.int32),
        ),
        scratch_shapes=[stage_type(capacity)],
    )(
        owner.reshape(1, blocks),
        req_module.reshape(1, rows),
        req_doc.reshape(1, rows),
        requests,
    )
    first_arrived = exchange(first_sent)

    token_count = tokens.shape[1]
    entries = HEADS * latent_count
    partial_rows = -(-(entries + 2 + tag_parts) // SUB) * SUB
    chunks = width // (SUB * LANES)
    depth = width // chunks
    partial = call(
        functools.partial(attend_kernel, chunks),
        "attend",
        vmem=60,
        in_specs=[in_hbm] * 3 + [in_vmem] * 2,
        out_shape=jax.ShapeDtypeStruct((partial_rows, head_dim), jnp.float32),
        scratch_shapes=[
            pltpu.VMEM((chunks, token_count, depth), jnp.bfloat16),
            pltpu.VMEM((chunks, depth, latent_width), jnp.bfloat16),
            pltpu.VMEM((chunks, depth, latent_width), jnp.bfloat16),
            pltpu.SemaphoreType.DMA((chunks, 3)),
        ],
    )(tokens, w_keys, w_values, latents, tags)
    packet_rows = latent_count + -(-ctx_count // SUB) * SUB
    packet = call(
        functools.partial(summary_kernel, tag_parts),
        "summarize",
        out_shape=jax.ShapeDtypeStruct((packet_rows, latent_width), jnp.bfloat16),
    )(lax.all_gather(partial, "ctx"), latents, w_out, latent_gain.reshape(1, latent_width))

    share = doc_count // ctx_count
    half = max(1, ctx_count // 2)
    order = [ctx // 2 + ctx % 2 * half for ctx in range(ctx_count)]
    fetched = []
    for turn in range(share):
        pairs = [
            (doc * ctx_count + ctx, (doc ^ (order[ctx] * share + turn)) * ctx_count + ctx)
            for doc in range(doc_count)
            for ctx in range(ctx_count)
        ]
        fetched.append(lax.ppermute(packet, ALL, pairs))
    second_arrived = exchange(after(second_sent, *fetched))
    gathered = lax.all_gather(jnp.stack(fetched), "ctx")
    everyone = jnp.stack([gathered[order.index(part)] for part in range(ctx_count)]).reshape(
        doc_count, packet_rows, latent_width
    )

    def tag_type(slot_count):
        return jax.ShapeDtypeStruct((slot_count * blocks, 1), jnp.int32)

    factor_type = jax.ShapeDtypeStruct((doc_count * latent_count, width), jnp.bfloat16)
    long_columns = -(-LONG // (doc_count * latent_count) // LANES) * LANES
    long_type = jax.ShapeDtypeStruct(
        (doc_count * latent_count, max(width, long_columns)), jnp.bfloat16
    )
    down_factor, up_factor, first_tags, second_tags = call(
        functools.partial(factor_kernel, blocks, capacity, early, latent_count, chunks),
        "factors",
        vmem=60,
        in_specs=[in_smem, in_vmem, in_hbm, in_hbm],
        out_specs=(in_hbm, in_hbm, in_vmem, in_vmem),
        out_shape=(factor_type, long_type, tag_type(early), tag_type(late)),
        scratch_shapes=[
            pltpu.VMEM((chunks, 2, latent_width, depth), jnp.bfloat16),
            pltpu.VMEM((chunks, 2, doc_count * latent_count, depth), jnp.bfloat16),
            pltpu.SemaphoreType.DMA((chunks, 2)),
            pltpu.SemaphoreType.DMA((chunks, 2)),
        ],
    )(me, everyone, heads_down, heads_up)

    first_coeff = call(
        functools.partial(coeff_kernel, blocks, early, latent_count, ctx_count),
        "coefficients",
        in_specs=[in_smem] + [in_vmem] * 3,
        out_shape=jax.ShapeDtypeStruct(
            (early * blocks, doc_count * latent_count), jnp.bfloat16
        ),
        scratch_shapes=[stage_type(early)],
    )(me, first_tags, down_factor, first_arrived)
    update = call(
        functools.partial(update_kernel, blocks, capacity, latent_count, ctx_count),
        "update",
        in_specs=[in_smem] + [in_vmem] * 2 + [outside, in_vmem, in_vmem],
        out_shape=block_type(capacity),
        scratch_shapes=[
            stage_type(capacity),
            pltpu.VMEM(factor_type.shape, factor_type.dtype),
            pltpu.SemaphoreType.DMA,
        ],
    )(me, second_tags, down_factor, up_factor, first_coeff, second_arrived)
    returned = exchange(update)
    return call(
        functools.partial(finish_kernel, blocks, capacity),
        "finish_rows",
        out_specs=outside,
        out_shape=jax.ShapeDtypeStruct((rows, width), jnp.bfloat16),
        scratch_shapes=[
            pltpu.VMEM((SUB, rows, piece), jnp.bfloat16),
            stage_type(capacity),
            pltpu.SemaphoreType.DMA((SUB,)),
        ],
    )(returned, slots, requests)


def solution(mesh):
    in_specs = (
        P("doc", "ctx", None),
        P(),
        P(),
        P(),
        P(),
        P(),
        P(ALL, None, None),
        P(ALL, None, None),
        P(),
        P(ALL, None),
        P(ALL),
        P(ALL, None),
    )
    return jax.shard_map(
        on_device, mesh=mesh, in_specs=in_specs, out_specs=P(ALL, None), check_vma=False
    )
```

```python
import functools
import math

import jax
import jax.numpy as jnp
from jax import lax
from jax.experimental import pallas as pl
from jax.experimental.pallas import tpu as pltpu
from jax.sharding import PartitionSpec as P

HEADS = 4
SUB = 8
LANES = 128
LONG = 20 * 1024 * 1024
ALL = ("doc", "ctx")


def call(kernel, name, vmem=32, **options):
    return pl.pallas_call(
        kernel,
        name=name,
        compiler_params=pltpu.CompilerParams(vmem_limit_bytes=vmem * 1024 * 1024),
        **options,
    )


def scatter_pieces(stage, piece_index, values, blocks, capacity, piece):
    for slot in range(capacity):
        for lane in range(piece // LANES):
            stage[
                slot * (piece // LANES) + lane, pl.ds(piece_index, blocks, stride=SUB), :
            ] = values[slot * blocks : (slot + 1) * blocks, lane * LANES : (lane + 1) * LANES]


def gather_pieces(stage, piece_index, blocks, capacity, piece):
    return jnp.concatenate(
        [
            jnp.concatenate(
                [
                    stage[slot * (piece // LANES) + lane, pl.ds(piece_index, blocks, stride=SUB), :]
                    for lane in range(piece // LANES)
                ],
                axis=1,
            ).astype(jnp.bfloat16)
            for slot in range(capacity)
        ],
        axis=0,
    )


def fill_stage(stage, sources):
    start = 0
    for source in sources:
        for lane in range(source.shape[1] // LANES):
            stage[start] = source[:, lane * LANES : (lane + 1) * LANES].astype(jnp.float32)
            start += 1


def drain_stage(stage, targets):
    start = 0
    for target in targets:
        for lane in range(target.shape[1] // LANES):
            target[:, lane * LANES : (lane + 1) * LANES] = stage[start].astype(target.dtype)
            start += 1


def as_column(row):
    n = row.shape[1]
    on_diagonal = lax.broadcasted_iota(jnp.int32, (n, n), 0) == lax.broadcasted_iota(
        jnp.int32, (n, n), 1
    )
    return jnp.sum(jnp.where(on_diagonal, row, jnp.zeros_like(row)), axis=1, keepdims=True)


def as_row(column):
    n = column.shape[0]
    on_diagonal = lax.broadcasted_iota(jnp.int32, (n, n), 0) == lax.broadcasted_iota(
        jnp.int32, (n, n), 1
    )
    return jnp.sum(jnp.where(on_diagonal, column, jnp.zeros_like(column)), axis=0, keepdims=True)


def place_kernel(
    blocks,
    capacity,
    owners_outside,
    modules_outside,
    requests_outside,
    sent,
    slots,
    owner_row,
    module_row,
    requests,
    stage,
    done,
):
    rows, width = requests.shape
    piece = width // SUB
    copies = [
        pltpu.make_async_copy(source, target, done.at[number])
        for number, (source, target) in enumerate(
            (
                (owners_outside, owner_row),
                (modules_outside, module_row),
                (requests_outside, requests),
            )
        )
    ]
    for copy in copies:
        copy.start()
    copies[0].wait()
    copies[1].wait()
    modules = module_row[...]
    owners = as_column(owner_row[...])
    named = lax.broadcasted_iota(jnp.int32, (blocks, rows), 0) == modules
    target = jnp.sum(jnp.where(named, owners, 0), axis=0, keepdims=True)
    first = lax.broadcasted_iota(jnp.int32, (rows, rows), 0)
    second = lax.broadcasted_iota(jnp.int32, (rows, rows), 1)
    ahead = (as_column(modules) == modules) & (first < second)
    rank = jnp.sum(ahead.astype(jnp.int32), axis=0, keepdims=True)
    slot_row = rank * blocks + target
    slots[...] = slot_row
    slot_ids = lax.broadcasted_iota(jnp.int32, (capacity * blocks, rows), 0)
    placer = (slot_ids == slot_row).astype(jnp.float32).astype(jnp.bfloat16)
    copies[2].wait()
    for index in range(SUB):
        moved = jnp.dot(
            placer,
            requests[:, index * piece : (index + 1) * piece],
            preferred_element_type=jnp.float32,
        )
        scatter_pieces(stage, index, moved, blocks, capacity, piece)
    drain_stage(stage, (sent,))


def place_more_kernel(blocks, start, capacity, slots, requests, sent, stage):
    rows, width = requests.shape
    piece = width // SUB
    slot_ids = start * blocks + lax.broadcasted_iota(jnp.int32, (capacity * blocks, rows), 0)
    placer = (slot_ids == slots[...]).astype(jnp.float32).astype(jnp.bfloat16)
    for index in range(SUB):
        moved = jnp.dot(
            placer,
            requests[:, index * piece : (index + 1) * piece],
            preferred_element_type=jnp.float32,
        )
        scatter_pieces(stage, index, moved, blocks, capacity, piece)
    drain_stage(stage, (sent,))


def attend_kernel(
    chunks,
    tag_parts,
    tokens,
    w_keys,
    w_values,
    latents,
    slots,
    doc_row,
    partial,
    tokens_in,
    keys_in,
    values_in,
    done,
):
    depth = w_keys.shape[0] // chunks
    copies = []
    for chunk in range(chunks):
        part = pl.ds(chunk * depth, depth)
        copies.append(
            [
                pltpu.make_async_copy(
                    tokens.at[0, :, part], tokens_in.at[chunk], done.at[chunk, 0]
                ),
                pltpu.make_async_copy(w_keys.at[part, :], keys_in.at[chunk], done.at[chunk, 1]),
                pltpu.make_async_copy(w_values.at[part, :], values_in.at[chunk], done.at[chunk, 2]),
            ]
        )
    for group in copies:
        for copy in group:
            copy.start()
    keys = values = 0.0
    for chunk in range(chunks):
        for copy in copies[chunk]:
            copy.wait()
        keys = keys + jnp.dot(
            tokens_in[chunk], keys_in[chunk], preferred_element_type=jnp.float32
        )
        values = values + jnp.dot(
            tokens_in[chunk], values_in[chunk], preferred_element_type=jnp.float32
        )
    latent_count, width = latents.shape
    head_dim = width // HEADS
    queries = latents[...].astype(jnp.bfloat16)
    key_rows = keys.astype(jnp.bfloat16)
    value_rows = values.astype(jnp.bfloat16).astype(jnp.float32)
    peaks, sums = [], []
    for head in range(HEADS):
        lanes = slice(head * head_dim, (head + 1) * head_dim)
        scores = lax.dot_general(
            queries[:, lanes],
            key_rows[:, lanes],
            (((1,), (1,)), ((), ())),
            preferred_element_type=jnp.float32,
        ) / math.sqrt(head_dim)
        peak = jnp.max(scores, axis=1, keepdims=True)
        expo = jnp.exp(scores - peak)
        peaks.append(peak)
        sums.append(jnp.sum(expo, axis=1, keepdims=True))
        partial[head * latent_count : (head + 1) * latent_count, :] = jnp.dot(
            expo,
            value_rows[:, lanes],
            precision=lax.Precision.HIGHEST,
            preferred_element_type=jnp.float32,
        )
    entries = HEADS * latent_count
    partial[entries:, :] = jnp.zeros_like(partial[entries:, :])
    partial[entries : entries + 1, :entries] = as_row(jnp.concatenate(peaks, axis=0))
    partial[entries + 1 : entries + 2, :entries] = as_row(jnp.concatenate(sums, axis=0))
    slot_column = as_column(slots[...])
    documents = as_column(doc_row[...] + 1)
    for part in range(tag_parts):
        lanes = lax.broadcasted_iota(jnp.int32, (slot_column.shape[0], LANES), 1) + part * LANES
        partial[entries + 2 + part : entries + 3 + part, :] = jnp.sum(
            jnp.where(lanes == slot_column, documents, 0), axis=0, keepdims=True
        ).astype(jnp.float32)


def summary_kernel(tag_parts, pieces, latents, w_out, gain, packet):
    members = pieces.shape[0]
    latent_count, width = latents.shape
    entries = HEADS * latent_count
    peaks = [as_column(pieces[c, entries : entries + 1, :entries]) for c in range(members)]
    summit = functools.reduce(jnp.maximum, peaks)
    total, weighted = 0.0, 0.0
    for c in range(members):
        ratio = jnp.exp(peaks[c] - summit)
        total = total + as_column(pieces[c, entries + 1 : entries + 2, :entries]) * ratio
        weighted = weighted + pieces[c, :entries, :] * ratio
    attended = weighted / total
    attended = jnp.concatenate(
        [attended[h * latent_count : (h + 1) * latent_count] for h in range(HEADS)], axis=1
    ).astype(jnp.bfloat16)
    mixed = latents[...] + jnp.dot(attended, w_out[...], preferred_element_type=jnp.float32)
    summary = (
        mixed
        * lax.rsqrt(jnp.mean(mixed * mixed, axis=1, keepdims=True) + 1e-06)
        * gain[...]
    )
    packet[:latent_count, :] = summary.astype(jnp.bfloat16)
    tag_rows = [
        jnp.concatenate(
            [pieces[c, entries + 2 + part : entries + 3 + part, :] for part in range(tag_parts)],
            axis=1,
        )
        for c in range(members)
    ]
    block = jnp.concatenate(tag_rows, axis=0)
    block = jnp.pad(
        block,
        ((0, packet.shape[0] - latent_count - members), (0, width - tag_parts * LANES)),
    )
    packet[latent_count:, :] = block.astype(jnp.bfloat16)


def factor_kernel(
    blocks,
    capacity,
    early,
    latent_count,
    chunks,
    me,
    everyone,
    heads_down,
    heads_up,
    down,
    up,
    tags_first,
    tags_second,
    heads_in,
    factors_out,
    arrived,
    left,
):
    depth = down.shape[1] // chunks
    jobs = []
    for chunk in range(chunks):
        part = pl.ds(chunk * depth, depth)
        for side, (heads, factor) in enumerate(((heads_down, down), (heads_up, up))):
            jobs.append(
                (
                    chunk,
                    side,
                    pltpu.make_async_copy(
                        heads.at[0, :, part], heads_in.at[chunk, side], arrived.at[chunk, side]
                    ),
                    pltpu.make_async_copy(
                        factors_out.at[chunk, side], factor.at[:, part], left.at[chunk, side]
                    ),
                )
            )
    for job in jobs:
        job[2].start()
    documents = everyone.shape[0]
    members = blocks // documents
    summaries = jnp.concatenate([everyone[x, :latent_count, :] for x in range(documents)], axis=0)
    device = me[0, 0]
    my_doc = device // members
    by_entry = jnp.concatenate(
        [
            everyone[x, latent_count : latent_count + members, :].astype(jnp.float32)
            for x in range(documents)
        ],
        axis=0,
    ).astype(jnp.bfloat16)
    source = lax.broadcasted_iota(jnp.int32, (blocks, blocks), 0)
    entry = lax.broadcasted_iota(jnp.int32, (blocks, blocks), 1)
    sorter = source == ((entry // members) ^ my_doc) * members + entry % members
    sorter = sorter.astype(jnp.float32).astype(jnp.bfloat16)
    arranged = jnp.dot(sorter, by_entry, preferred_element_type=jnp.float32)
    lanes = lax.broadcasted_iota(jnp.int32, arranged.shape, 1)
    for slot in range(capacity):
        column = jnp.sum(
            jnp.where(lanes == slot * blocks + device, arranged, 0.0), axis=1, keepdims=True
        ).astype(jnp.int32)
        target, position = (tags_first, slot) if slot < early else (tags_second, slot - early)
        target[position * blocks : (position + 1) * blocks, :] = column
    for chunk, side, arriving, leaving in jobs:
        arriving.wait()
        factors_out[chunk, side] = jnp.dot(
            summaries, heads_in[chunk, side], preferred_element_type=jnp.float32
        ).astype(jnp.bfloat16)
        leaving.start()
    for job in jobs:
        job[3].wait()


def coeff_kernel(blocks, capacity, latent_count, members, me, tags, down, arrived, *refs):
    coeff_out, stage = refs
    coeff_out[...] = coefficients(
        blocks, capacity, latent_count, members, me, tags, down, arrived, stage
    )


def coefficients(
    blocks, capacity, latent_count, members, me, tags, down, arrived, stage
):
    width = down.shape[1]
    piece = width // SUB
    for lane in range(capacity * piece // LANES):
        stage[lane] = arrived[:, lane * LANES : (lane + 1) * LANES].astype(jnp.float32)
    coeff = 0.0
    for index in range(SUB):
        coeff = coeff + lax.dot_general(
            gather_pieces(stage, index, blocks, capacity, piece),
            down[:, index * piece : (index + 1) * piece],
            (((1,), (1,)), ((), ())),
            preferred_element_type=jnp.float32,
        )
    column_doc = (
        lax.broadcasted_iota(jnp.int32, coeff.shape, 1) // latent_count
    ) ^ (me[0, 0] // members)
    matched = tags[...] - 1 == column_doc
    return jnp.where(matched, coeff / math.sqrt(width), 0.0).astype(jnp.bfloat16)


def update_kernel(
    blocks, capacity, latent_count, members, me, tags, down, up, first_coeff, arrived, *refs
):
    update, stage, up_in, up_done = refs
    piece = down.shape[1] // SUB
    late = arrived.shape[1] // piece
    up_copy = pltpu.make_async_copy(up.at[:, pl.ds(0, down.shape[1])], up_in, up_done)
    up_copy.start()
    coeff = coefficients(
        blocks, late, latent_count, members, me, tags, down, arrived, stage
    )
    coeff = jnp.concatenate([first_coeff[...], coeff], axis=0)
    up_copy.wait()
    for index in range(SUB):
        moved = jnp.dot(
            coeff, up_in[:, index * piece : (index + 1) * piece], preferred_element_type=jnp.float32
        ) * (1.0 / math.sqrt(latent_count))
        scatter_pieces(stage, index, moved, blocks, capacity, piece)
    drain_stage(stage, (update,))


def finish_kernel(blocks, capacity, returned, slots, requests, adapted, adapted_out, stage, done):
    rows, width = requests.shape
    piece = width // SUB
    fill_stage(stage, (returned,))
    slot_column = as_column(slots[...])
    wanted = lax.broadcasted_iota(jnp.int32, (rows, capacity * blocks), 1) == slot_column
    picker = wanted.astype(jnp.float32).astype(jnp.bfloat16)
    leaving = []
    for index in range(SUB):
        gathered = jnp.dot(
            picker,
            gather_pieces(stage, index, blocks, capacity, piece),
            preferred_element_type=jnp.float32,
        )
        adapted_out[index] = (
            requests[:, index * piece : (index + 1) * piece].astype(jnp.float32) + gathered
        ).astype(adapted.dtype)
        leaving.append(
            pltpu.make_async_copy(
                adapted_out.at[index], adapted.at[:, pl.ds(index * piece, piece)], done.at[index]
            )
        )
        leaving[index].start()
    for copy in leaving:
        copy.wait()


def on_device(
    tokens,
    latents,
    w_keys,
    w_values,
    w_out,
    latent_gain,
    heads_down,
    heads_up,
    owner,
    requests,
    req_doc,
    req_module,
):
    doc_count = lax.axis_size("doc")
    ctx_count = lax.axis_size("ctx")
    blocks = doc_count * ctx_count
    rows, width = requests.shape
    capacity = max(2, rows // blocks + 1)
    piece = width // SUB
    latent_count, latent_width = latents.shape
    head_dim = latent_width // HEADS
    my_doc = lax.axis_index("doc")
    my_ctx = lax.axis_index("ctx")
    early = max(1, (capacity - 1) // 2)
    late = capacity - early
    tag_parts = -(-(capacity * blocks) // LANES)
    me = (my_doc * ctx_count + my_ctx).astype(jnp.int32).reshape(1, 1)
    in_smem = pl.BlockSpec(memory_space=pltpu.SMEM)
    in_vmem = pl.BlockSpec(memory_space=pltpu.VMEM)
    in_hbm = pl.BlockSpec(memory_space=pl.ANY)
    outside = pl.BlockSpec(memory_space=pltpu.HBM)

    def after(values, *others):
        return lax.optimization_barrier((values, *others))[0]

    def block_type(slot_count):
        return jax.ShapeDtypeStruct((blocks * SUB, slot_count * piece), jnp.bfloat16)

    def stage_type(slot_count):
        return pltpu.VMEM((slot_count * piece // LANES, blocks * SUB, LANES), jnp.float32)

    def exchange(values):
        return lax.all_to_all(
            values.reshape(blocks, SUB, -1), ALL, split_axis=0, concat_axis=0, tiled=True
        ).reshape(values.shape)

    first_sent, slots = call(
        functools.partial(place_kernel, blocks, early),
        "place_rows",
        vmem=60,
        in_specs=[outside] * 3,
        out_shape=(
            block_type(early),
            jax.ShapeDtypeStruct((1, rows), jnp.int32),
        ),
        scratch_shapes=[
            pltpu.VMEM((1, blocks), jnp.int32),
            pltpu.VMEM((1, rows), jnp.int32),
            pltpu.VMEM((rows, width), jnp.bfloat16),
            stage_type(early),
            pltpu.SemaphoreType.DMA((3,)),
        ],
    )(
        owner.reshape(1, blocks),
        req_module.reshape(1, rows),
        requests,
    )
    first_arrived = exchange(first_sent)

    token_count = tokens.shape[1]
    entries = HEADS * latent_count
    partial_rows = -(-(entries + 2 + tag_parts) // SUB) * SUB
    chunks = width // (SUB * LANES)
    depth = width // chunks
    partial = call(
        functools.partial(attend_kernel, chunks, tag_parts),
        "attend",
        vmem=60,
        in_specs=[in_hbm] * 3 + [in_vmem] * 3,
        out_shape=jax.ShapeDtypeStruct((partial_rows, head_dim), jnp.float32),
        scratch_shapes=[
            pltpu.VMEM((chunks, token_count, depth), jnp.bfloat16),
            pltpu.VMEM((chunks, depth, latent_width), jnp.bfloat16),
            pltpu.VMEM((chunks, depth, latent_width), jnp.bfloat16),
            pltpu.SemaphoreType.DMA((chunks, 3)),
        ],
    )(tokens, w_keys, w_values, latents, slots, req_doc.reshape(1, rows))
    packet_rows = latent_count + -(-ctx_count // SUB) * SUB
    packet = call(
        functools.partial(summary_kernel, tag_parts),
        "summarize",
        out_shape=jax.ShapeDtypeStruct((packet_rows, latent_width), jnp.bfloat16),
    )(lax.all_gather(partial, "ctx"), latents, w_out, latent_gain.reshape(1, latent_width))

    share = doc_count // ctx_count
    half = max(1, ctx_count // 2)
    order = [ctx // 2 + ctx % 2 * half for ctx in range(ctx_count)]
    fetched = []
    for turn in range(share):
        pairs = [
            (doc * ctx_count + ctx, (doc ^ (order[ctx] * share + turn)) * ctx_count + ctx)
            for doc in range(doc_count)
            for ctx in range(ctx_count)
        ]
        fetched.append(lax.ppermute(packet, ALL, pairs))
    second_sent = call(
        functools.partial(place_more_kernel, blocks, early, late),
        "place_more",
        vmem=60,
        out_shape=block_type(late),
        scratch_shapes=[stage_type(late)],
    )(after(slots, packet), requests)
    second_arrived = exchange(after(second_sent, *fetched))
    gathered = lax.all_gather(jnp.stack(fetched), "ctx")
    everyone = jnp.stack([gathered[order.index(part)] for part in range(ctx_count)]).reshape(
        doc_count, packet_rows, latent_width
    )

    def tag_type(slot_count):
        return jax.ShapeDtypeStruct((slot_count * blocks, 1), jnp.int32)

    factor_type = jax.ShapeDtypeStruct((doc_count * latent_count, width), jnp.bfloat16)
    long_columns = -(-LONG // (doc_count * latent_count) // LANES) * LANES
    long_type = jax.ShapeDtypeStruct(
        (doc_count * latent_count, max(width, long_columns)), jnp.bfloat16
    )
    down_factor, up_factor, first_tags, second_tags = call(
        functools.partial(factor_kernel, blocks, capacity, early, latent_count, chunks),
        "factors",
        vmem=60,
        in_specs=[in_smem, in_vmem, in_hbm, in_hbm],
        out_specs=(in_hbm, in_hbm, in_vmem, in_vmem),
        out_shape=(factor_type, long_type, tag_type(early), tag_type(late)),
        scratch_shapes=[
            pltpu.VMEM((chunks, 2, latent_width, depth), jnp.bfloat16),
            pltpu.VMEM((chunks, 2, doc_count * latent_count, depth), jnp.bfloat16),
            pltpu.SemaphoreType.DMA((chunks, 2)),
            pltpu.SemaphoreType.DMA((chunks, 2)),
        ],
    )(me, everyone, heads_down, heads_up)

    first_coeff = call(
        functools.partial(coeff_kernel, blocks, early, latent_count, ctx_count),
        "coefficients",
        in_specs=[in_smem] + [in_vmem] * 3,
        out_shape=jax.ShapeDtypeStruct(
            (early * blocks, doc_count * latent_count), jnp.bfloat16
        ),
        scratch_shapes=[stage_type(early)],
    )(me, first_tags, down_factor, first_arrived)
    update = call(
        functools.partial(update_kernel, blocks, capacity, latent_count, ctx_count),
        "update",
        in_specs=[in_smem] + [in_vmem] * 2 + [outside, in_vmem, in_vmem],
        out_shape=block_type(capacity),
        scratch_shapes=[
            stage_type(capacity),
            pltpu.VMEM(factor_type.shape, factor_type.dtype),
            pltpu.SemaphoreType.DMA,
        ],
    )(me, second_tags, down_factor, up_factor, first_coeff, second_arrived)
    returned = exchange(update)
    return call(
        functools.partial(finish_kernel, blocks, capacity),
        "finish_rows",
        out_specs=outside,
        out_shape=jax.ShapeDtypeStruct((rows, width), jnp.bfloat16),
        scratch_shapes=[
            pltpu.VMEM((SUB, rows, piece), jnp.bfloat16),
            stage_type(capacity),
            pltpu.SemaphoreType.DMA((SUB,)),
        ],
    )(returned, slots, requests)


def solution(mesh):
    in_specs = (
        P("doc", "ctx", None),
        P(),
        P(),
        P(),
        P(),
        P(),
        P(ALL, None, None),
        P(ALL, None, None),
        P(),
        P(ALL, None),
        P(ALL),
        P(ALL, None),
    )
    return jax.shard_map(
        on_device, mesh=mesh, in_specs=in_specs, out_specs=P(ALL, None), check_vma=False
    )
```

```python
import functools
import math

import jax
import jax.numpy as jnp
from jax import lax
from jax.experimental import pallas as pl
from jax.experimental.pallas import tpu as pltpu
from jax.sharding import PartitionSpec as P

HEADS = 4
SUB = 8
LANES = 128
LONG = 20 * 1024 * 1024
ALL = ("doc", "ctx")


def call(kernel, name, vmem=32, **options):
    return pl.pallas_call(
        kernel,
        name=name,
        compiler_params=pltpu.CompilerParams(vmem_limit_bytes=vmem * 1024 * 1024),
        **options,
    )


def scatter_pieces(stage, piece_index, values, blocks, capacity, piece):
    for slot in range(capacity):
        for lane in range(piece // LANES):
            stage[
                slot * (piece // LANES) + lane, pl.ds(piece_index, blocks, stride=SUB), :
            ] = values[slot * blocks : (slot + 1) * blocks, lane * LANES : (lane + 1) * LANES]


def gather_pieces(stage, piece_index, blocks, capacity, piece):
    return jnp.concatenate(
        [
            jnp.concatenate(
                [
                    stage[slot * (piece // LANES) + lane, pl.ds(piece_index, blocks, stride=SUB), :]
                    for lane in range(piece // LANES)
                ],
                axis=1,
            ).astype(jnp.bfloat16)
            for slot in range(capacity)
        ],
        axis=0,
    )


def fill_stage(stage, sources):
    start = 0
    for source in sources:
        for lane in range(source.shape[1] // LANES):
            stage[start] = source[:, lane * LANES : (lane + 1) * LANES].astype(jnp.float32)
            start += 1


def drain_stage(stage, targets):
    start = 0
    for target in targets:
        for lane in range(target.shape[1] // LANES):
            target[:, lane * LANES : (lane + 1) * LANES] = stage[start].astype(target.dtype)
            start += 1


def as_column(row):
    n = row.shape[1]
    on_diagonal = lax.broadcasted_iota(jnp.int32, (n, n), 0) == lax.broadcasted_iota(
        jnp.int32, (n, n), 1
    )
    return jnp.sum(jnp.where(on_diagonal, row, jnp.zeros_like(row)), axis=1, keepdims=True)


def as_row(column):
    n = column.shape[0]
    on_diagonal = lax.broadcasted_iota(jnp.int32, (n, n), 0) == lax.broadcasted_iota(
        jnp.int32, (n, n), 1
    )
    return jnp.sum(jnp.where(on_diagonal, column, jnp.zeros_like(column)), axis=0, keepdims=True)


def place_kernel(
    blocks,
    capacity,
    owners_outside,
    modules_outside,
    requests_outside,
    sent,
    slots,
    owner_row,
    module_row,
    requests,
    stage,
    done,
):
    rows, width = requests.shape
    piece = width // SUB
    copies = [
        pltpu.make_async_copy(source, target, done.at[number])
        for number, (source, target) in enumerate(
            (
                (owners_outside, owner_row),
                (modules_outside, module_row),
                (requests_outside, requests),
            )
        )
    ]
    for copy in copies:
        copy.start()
    copies[0].wait()
    copies[1].wait()
    modules = module_row[...]
    owners = as_column(owner_row[...])
    named = lax.broadcasted_iota(jnp.int32, (blocks, rows), 0) == modules
    target = jnp.sum(jnp.where(named, owners, 0), axis=0, keepdims=True)
    first = lax.broadcasted_iota(jnp.int32, (rows, rows), 0)
    second = lax.broadcasted_iota(jnp.int32, (rows, rows), 1)
    ahead = (as_column(modules) == modules) & (first < second)
    rank = jnp.sum(ahead.astype(jnp.int32), axis=0, keepdims=True)
    slot_row = rank * blocks + target
    slots[...] = slot_row
    slot_ids = lax.broadcasted_iota(jnp.int32, (capacity * blocks, rows), 0)
    placer = (slot_ids == slot_row).astype(jnp.float32).astype(jnp.bfloat16)
    copies[2].wait()
    for index in range(SUB):
        moved = jnp.dot(
            placer,
            requests[:, index * piece : (index + 1) * piece],
            preferred_element_type=jnp.float32,
        )
        scatter_pieces(stage, index, moved, blocks, capacity, piece)
    drain_stage(stage, (sent,))


def place_more_kernel(blocks, start, capacity, slots, requests, sent, stage):
    rows, width = requests.shape
    piece = width // SUB
    slot_ids = start * blocks + lax.broadcasted_iota(jnp.int32, (capacity * blocks, rows), 0)
    placer = (slot_ids == slots[...]).astype(jnp.float32).astype(jnp.bfloat16)
    for index in range(SUB):
        moved = jnp.dot(
            placer,
            requests[:, index * piece : (index + 1) * piece],
            preferred_element_type=jnp.float32,
        )
        scatter_pieces(stage, index, moved, blocks, capacity, piece)
    drain_stage(stage, (sent,))


def attend_kernel(
    chunks,
    tag_parts,
    tokens,
    w_keys,
    w_values,
    latents,
    slots,
    doc_row,
    partial,
    tokens_in,
    keys_in,
    values_in,
    done,
):
    depth = w_keys.shape[0] // chunks
    copies = []
    for chunk in range(chunks):
        part = pl.ds(chunk * depth, depth)
        copies.append(
            [
                pltpu.make_async_copy(
                    tokens.at[0, :, part], tokens_in.at[chunk], done.at[chunk, 0]
                ),
                pltpu.make_async_copy(w_keys.at[part, :], keys_in.at[chunk], done.at[chunk, 1]),
                pltpu.make_async_copy(w_values.at[part, :], values_in.at[chunk], done.at[chunk, 2]),
            ]
        )
    for group in copies:
        for copy in group:
            copy.start()
    keys = values = 0.0
    for chunk in range(chunks):
        for copy in copies[chunk]:
            copy.wait()
        keys = keys + jnp.dot(
            tokens_in[chunk], keys_in[chunk], preferred_element_type=jnp.float32
        )
        values = values + jnp.dot(
            tokens_in[chunk], values_in[chunk], preferred_element_type=jnp.float32
        )
    latent_count, width = latents.shape
    head_dim = width // HEADS
    queries = latents[...].astype(jnp.bfloat16)
    key_rows = keys.astype(jnp.bfloat16)
    value_rows = values.astype(jnp.bfloat16).astype(jnp.float32)
    peaks, sums = [], []
    for head in range(HEADS):
        lanes = slice(head * head_dim, (head + 1) * head_dim)
        scores = lax.dot_general(
            queries[:, lanes],
            key_rows[:, lanes],
            (((1,), (1,)), ((), ())),
            preferred_element_type=jnp.float32,
        ) / math.sqrt(head_dim)
        peak = jnp.max(scores, axis=1, keepdims=True)
        expo = jnp.exp(scores - peak)
        peaks.append(peak)
        sums.append(jnp.sum(expo, axis=1, keepdims=True))
        partial[head * latent_count : (head + 1) * latent_count, :] = jnp.dot(
            expo,
            value_rows[:, lanes],
            precision=lax.Precision.HIGHEST,
            preferred_element_type=jnp.float32,
        )
    entries = HEADS * latent_count
    partial[entries:, :] = jnp.zeros_like(partial[entries:, :])
    partial[entries : entries + 1, :entries] = as_row(jnp.concatenate(peaks, axis=0))
    partial[entries + 1 : entries + 2, :entries] = as_row(jnp.concatenate(sums, axis=0))
    slot_column = as_column(slots[...])
    documents = as_column(doc_row[...] + 1)
    for part in range(tag_parts):
        lanes = lax.broadcasted_iota(jnp.int32, (slot_column.shape[0], LANES), 1) + part * LANES
        partial[entries + 2 + part : entries + 3 + part, :] = jnp.sum(
            jnp.where(lanes == slot_column, documents, 0), axis=0, keepdims=True
        ).astype(jnp.float32)


def summary_kernel(tag_parts, pieces, latents, w_out, gain, packet):
    members = pieces.shape[0]
    latent_count, width = latents.shape
    entries = HEADS * latent_count
    peaks = [as_column(pieces[c, entries : entries + 1, :entries]) for c in range(members)]
    summit = functools.reduce(jnp.maximum, peaks)
    total, weighted = 0.0, 0.0
    for c in range(members):
        ratio = jnp.exp(peaks[c] - summit)
        total = total + as_column(pieces[c, entries + 1 : entries + 2, :entries]) * ratio
        weighted = weighted + pieces[c, :entries, :] * ratio
    attended = weighted / total
    attended = jnp.concatenate(
        [attended[h * latent_count : (h + 1) * latent_count] for h in range(HEADS)], axis=1
    ).astype(jnp.bfloat16)
    mixed = latents[...] + jnp.dot(attended, w_out[...], preferred_element_type=jnp.float32)
    summary = (
        mixed
        * lax.rsqrt(jnp.mean(mixed * mixed, axis=1, keepdims=True) + 1e-06)
        * gain[...]
    )
    packet[:latent_count, :] = summary.astype(jnp.bfloat16)
    tag_rows = [
        jnp.concatenate(
            [pieces[c, entries + 2 + part : entries + 3 + part, :] for part in range(tag_parts)],
            axis=1,
        )
        for c in range(members)
    ]
    block = jnp.concatenate(tag_rows, axis=0)
    block = jnp.pad(
        block,
        ((0, packet.shape[0] - latent_count - members), (0, width - tag_parts * LANES)),
    )
    packet[latent_count:, :] = block.astype(jnp.bfloat16)


def factor_kernel(
    blocks,
    capacity,
    early,
    latent_count,
    chunks,
    me,
    everyone,
    heads_down,
    heads_up,
    down,
    up,
    tags_first,
    tags_second,
    heads_in,
    factors_out,
    arrived,
    left,
):
    depth = down.shape[1] // chunks
    jobs = []
    for chunk in range(chunks):
        part = pl.ds(chunk * depth, depth)
        for side, (heads, factor) in enumerate(((heads_down, down), (heads_up, up))):
            jobs.append(
                (
                    chunk,
                    side,
                    pltpu.make_async_copy(
                        heads.at[0, :, part], heads_in.at[chunk, side], arrived.at[chunk, side]
                    ),
                    pltpu.make_async_copy(
                        factors_out.at[chunk, side], factor.at[:, part], left.at[chunk, side]
                    ),
                )
            )
    for job in jobs:
        job[2].start()
    documents = everyone.shape[0]
    members = blocks // documents
    summaries = jnp.concatenate([everyone[x, :latent_count, :] for x in range(documents)], axis=0)
    device = me[0, 0]
    my_doc = device // members
    by_entry = jnp.concatenate(
        [everyone[x, latent_count:, :].astype(jnp.float32)[:members] for x in range(documents)],
        axis=0,
    ).astype(jnp.bfloat16)
    source = lax.broadcasted_iota(jnp.int32, (blocks, blocks), 0)
    entry = lax.broadcasted_iota(jnp.int32, (blocks, blocks), 1)
    sorter = source == ((entry // members) ^ my_doc) * members + entry % members
    sorter = sorter.astype(jnp.float32).astype(jnp.bfloat16)
    arranged = jnp.dot(sorter, by_entry, preferred_element_type=jnp.float32)
    lanes = lax.broadcasted_iota(jnp.int32, arranged.shape, 1)
    for slot in range(capacity):
        column = jnp.sum(
            jnp.where(lanes == slot * blocks + device, arranged, 0.0), axis=1, keepdims=True
        ).astype(jnp.int32)
        target, position = (tags_first, slot) if slot < early else (tags_second, slot - early)
        target[position * blocks : (position + 1) * blocks, :] = column
    for chunk, side, arriving, leaving in jobs:
        arriving.wait()
        factors_out[chunk, side] = jnp.dot(
            summaries, heads_in[chunk, side], preferred_element_type=jnp.float32
        ).astype(jnp.bfloat16)
        leaving.start()
    for job in jobs:
        job[3].wait()


def coeff_kernel(blocks, capacity, latent_count, members, me, tags, down, arrived, *refs):
    coeff_out, stage = refs
    coeff_out[...] = coefficients(
        blocks, capacity, latent_count, members, me, tags, down, arrived, stage
    )


def coefficients(
    blocks, capacity, latent_count, members, me, tags, down, arrived, stage
):
    width = down.shape[1]
    piece = width // SUB
    for lane in range(capacity * piece // LANES):
        stage[lane] = arrived[:, lane * LANES : (lane + 1) * LANES].astype(jnp.float32)
    coeff = 0.0
    for index in range(SUB):
        coeff = coeff + lax.dot_general(
            gather_pieces(stage, index, blocks, capacity, piece),
            down[:, index * piece : (index + 1) * piece],
            (((1,), (1,)), ((), ())),
            preferred_element_type=jnp.float32,
        )
    column_doc = (
        lax.broadcasted_iota(jnp.int32, coeff.shape, 1) // latent_count
    ) ^ (me[0, 0] // members)
    matched = tags[...] - 1 == column_doc
    return jnp.where(matched, coeff / math.sqrt(width), 0.0).astype(jnp.bfloat16)


def update_kernel(
    blocks, capacity, latent_count, members, me, tags, down, up, first_coeff, arrived, *refs
):
    update, stage, up_in, up_done = refs
    piece = down.shape[1] // SUB
    late = arrived.shape[1] // piece
    up_copy = pltpu.make_async_copy(up.at[:, pl.ds(0, down.shape[1])], up_in, up_done)
    up_copy.start()
    coeff = coefficients(
        blocks, late, latent_count, members, me, tags, down, arrived, stage
    )
    coeff = jnp.concatenate([first_coeff[...], coeff], axis=0)
    up_copy.wait()
    for index in range(SUB):
        moved = jnp.dot(
            coeff, up_in[:, index * piece : (index + 1) * piece], preferred_element_type=jnp.float32
        ) * (1.0 / math.sqrt(latent_count))
        scatter_pieces(stage, index, moved, blocks, capacity, piece)
    drain_stage(stage, (update,))


def finish_kernel(blocks, capacity, returned, slots, requests, adapted, adapted_out, stage, done):
    rows, width = requests.shape
    piece = width // SUB
    fill_stage(stage, (returned,))
    slot_column = as_column(slots[...])
    wanted = lax.broadcasted_iota(jnp.int32, (rows, capacity * blocks), 1) == slot_column
    picker = wanted.astype(jnp.float32).astype(jnp.bfloat16)
    leaving = []
    for index in range(SUB):
        gathered = jnp.dot(
            picker,
            gather_pieces(stage, index, blocks, capacity, piece),
            preferred_element_type=jnp.float32,
        )
        adapted_out[index] = (
            requests[:, index * piece : (index + 1) * piece].astype(jnp.float32) + gathered
        ).astype(adapted.dtype)
        leaving.append(
            pltpu.make_async_copy(
                adapted_out.at[index], adapted.at[:, pl.ds(index * piece, piece)], done.at[index]
            )
        )
        leaving[index].start()
    for copy in leaving:
        copy.wait()


def on_device(
    tokens,
    latents,
    w_keys,
    w_values,
    w_out,
    latent_gain,
    heads_down,
    heads_up,
    owner,
    requests,
    req_doc,
    req_module,
):
    doc_count = lax.axis_size("doc")
    ctx_count = lax.axis_size("ctx")
    blocks = doc_count * ctx_count
    rows, width = requests.shape
    capacity = max(2, rows // blocks + 1)
    piece = width // SUB
    latent_count, latent_width = latents.shape
    head_dim = latent_width // HEADS
    my_doc = lax.axis_index("doc")
    my_ctx = lax.axis_index("ctx")
    early = max(1, (capacity - 1) // 2)
    late = capacity - early
    tag_parts = -(-(capacity * blocks) // LANES)
    me = (my_doc * ctx_count + my_ctx).astype(jnp.int32).reshape(1, 1)
    in_smem = pl.BlockSpec(memory_space=pltpu.SMEM)
    in_vmem = pl.BlockSpec(memory_space=pltpu.VMEM)
    in_hbm = pl.BlockSpec(memory_space=pl.ANY)
    outside = pl.BlockSpec(memory_space=pltpu.HBM)

    def after(values, *others):
        return lax.optimization_barrier((values, *others))[0]

    def block_type(slot_count):
        return jax.ShapeDtypeStruct((blocks * SUB, slot_count * piece), jnp.bfloat16)

    def stage_type(slot_count):
        return pltpu.VMEM((slot_count * piece // LANES, blocks * SUB, LANES), jnp.float32)

    def exchange(values):
        return lax.all_to_all(
            values.reshape(blocks, SUB, -1), ALL, split_axis=0, concat_axis=0, tiled=True
        ).reshape(values.shape)

    first_sent, slots = call(
        functools.partial(place_kernel, blocks, early),
        "place_rows",
        vmem=60,
        in_specs=[outside] * 3,
        out_shape=(
            block_type(early),
            jax.ShapeDtypeStruct((1, rows), jnp.int32),
        ),
        scratch_shapes=[
            pltpu.VMEM((1, blocks), jnp.int32),
            pltpu.VMEM((1, rows), jnp.int32),
            pltpu.VMEM((rows, width), jnp.bfloat16),
            stage_type(early),
            pltpu.SemaphoreType.DMA((3,)),
        ],
    )(
        owner.reshape(1, blocks),
        req_module.reshape(1, rows),
        requests,
    )
    first_arrived = exchange(first_sent)

    token_count = tokens.shape[1]
    entries = HEADS * latent_count
    partial_rows = -(-(entries + 2 + tag_parts) // SUB) * SUB
    chunks = width // (SUB * LANES)
    depth = width // chunks
    partial = call(
        functools.partial(attend_kernel, chunks, tag_parts),
        "attend",
        vmem=60,
        in_specs=[in_hbm] * 3 + [in_vmem] * 3,
        out_shape=jax.ShapeDtypeStruct((partial_rows, head_dim), jnp.float32),
        scratch_shapes=[
            pltpu.VMEM((chunks, token_count, depth), jnp.bfloat16),
            pltpu.VMEM((chunks, depth, latent_width), jnp.bfloat16),
            pltpu.VMEM((chunks, depth, latent_width), jnp.bfloat16),
            pltpu.SemaphoreType.DMA((chunks, 3)),
        ],
    )(tokens, w_keys, w_values, latents, slots, req_doc.reshape(1, rows))
    packet_rows = latent_count + -(-ctx_count // 16) * 16
    packet = call(
        functools.partial(summary_kernel, tag_parts),
        "summarize",
        out_shape=jax.ShapeDtypeStruct((packet_rows, latent_width), jnp.bfloat16),
    )(lax.all_gather(partial, "ctx"), latents, w_out, latent_gain.reshape(1, latent_width))

    share = doc_count // ctx_count
    half = max(1, ctx_count // 2)
    order = [ctx // 2 + ctx % 2 * half for ctx in range(ctx_count)]
    fetched = []
    for turn in range(share):
        pairs = [
            (doc * ctx_count + ctx, (doc ^ (order[ctx] * share + turn)) * ctx_count + ctx)
            for doc in range(doc_count)
            for ctx in range(ctx_count)
        ]
        fetched.append(lax.ppermute(packet, ALL, pairs))
    second_sent = call(
        functools.partial(place_more_kernel, blocks, early, late),
        "place_more",
        vmem=60,
        out_shape=block_type(late),
        scratch_shapes=[stage_type(late)],
    )(after(slots, packet), requests)
    second_arrived = exchange(after(second_sent, *fetched))
    gathered = lax.all_gather(jnp.stack(fetched), "ctx")
    everyone = jnp.stack([gathered[order.index(part)] for part in range(ctx_count)]).reshape(
        doc_count, packet_rows, latent_width
    )

    def tag_type(slot_count):
        return jax.ShapeDtypeStruct((slot_count * blocks, 1), jnp.int32)

    factor_type = jax.ShapeDtypeStruct((doc_count * latent_count, width), jnp.bfloat16)
    long_columns = -(-LONG // (doc_count * latent_count) // LANES) * LANES
    long_type = jax.ShapeDtypeStruct(
        (doc_count * latent_count, max(width, long_columns)), jnp.bfloat16
    )
    down_factor, up_factor, first_tags, second_tags = call(
        functools.partial(factor_kernel, blocks, capacity, early, latent_count, chunks),
        "factors",
        vmem=60,
        in_specs=[in_smem, in_vmem, in_hbm, in_hbm],
        out_specs=(in_hbm, in_hbm, in_vmem, in_vmem),
        out_shape=(factor_type, long_type, tag_type(early), tag_type(late)),
        scratch_shapes=[
            pltpu.VMEM((chunks, 2, latent_width, depth), jnp.bfloat16),
            pltpu.VMEM((chunks, 2, doc_count * latent_count, depth), jnp.bfloat16),
            pltpu.SemaphoreType.DMA((chunks, 2)),
            pltpu.SemaphoreType.DMA((chunks, 2)),
        ],
    )(me, everyone, heads_down, heads_up)

    first_coeff = call(
        functools.partial(coeff_kernel, blocks, early, latent_count, ctx_count),
        "coefficients",
        in_specs=[in_smem] + [in_vmem] * 3,
        out_shape=jax.ShapeDtypeStruct(
            (early * blocks, doc_count * latent_count), jnp.bfloat16
        ),
        scratch_shapes=[stage_type(early)],
    )(me, first_tags, down_factor, first_arrived)
    update = call(
        functools.partial(update_kernel, blocks, capacity, latent_count, ctx_count),
        "update",
        in_specs=[in_smem] + [in_vmem] * 2 + [outside, in_vmem, in_vmem],
        out_shape=block_type(capacity),
        scratch_shapes=[
            stage_type(capacity),
            pltpu.VMEM(factor_type.shape, factor_type.dtype),
            pltpu.SemaphoreType.DMA,
        ],
    )(me, second_tags, down_factor, up_factor, first_coeff, second_arrived)
    returned = exchange(update)
    return call(
        functools.partial(finish_kernel, blocks, capacity),
        "finish_rows",
        out_specs=outside,
        out_shape=jax.ShapeDtypeStruct((rows, width), jnp.bfloat16),
        scratch_shapes=[
            pltpu.VMEM((SUB, rows, piece), jnp.bfloat16),
            stage_type(capacity),
            pltpu.SemaphoreType.DMA((SUB,)),
        ],
    )(returned, slots, requests)


def solution(mesh):
    in_specs = (
        P("doc", "ctx", None),
        P(),
        P(),
        P(),
        P(),
        P(),
        P(ALL, None, None),
        P(ALL, None, None),
        P(),
        P(ALL, None),
        P(ALL),
        P(ALL, None),
    )
    return jax.shard_map(
        on_device, mesh=mesh, in_specs=in_specs, out_specs=P(ALL, None), check_vma=False
    )
```

```python
import functools
import math

import jax
import jax.numpy as jnp
from jax import lax
from jax.experimental import pallas as pl
from jax.experimental.pallas import tpu as pltpu
from jax.sharding import PartitionSpec as P

HEADS = 4
SUB = 8
LANES = 128
CHUNKS = 4
LONG = 20 * 1024 * 1024
ALL = ("doc", "ctx")


def call(kernel, name, vmem=32, **options):
    return pl.pallas_call(
        kernel,
        name=name,
        compiler_params=pltpu.CompilerParams(vmem_limit_bytes=vmem * 1024 * 1024),
        **options,
    )


def scatter_pieces(stage, piece_index, values, blocks, capacity, piece):
    for slot in range(capacity):
        for lane in range(piece // LANES):
            stage[
                slot * (piece // LANES) + lane, pl.ds(piece_index, blocks, stride=SUB), :
            ] = values[slot * blocks : (slot + 1) * blocks, lane * LANES : (lane + 1) * LANES]


def gather_pieces(stage, piece_index, blocks, capacity, piece):
    return jnp.concatenate(
        [
            jnp.concatenate(
                [
                    stage[slot * (piece // LANES) + lane, pl.ds(piece_index, blocks, stride=SUB), :]
                    for lane in range(piece // LANES)
                ],
                axis=1,
            ).astype(jnp.bfloat16)
            for slot in range(capacity)
        ],
        axis=0,
    )


def fill_stage(stage, sources):
    start = 0
    for source in sources:
        for lane in range(source.shape[1] // LANES):
            stage[start] = source[:, lane * LANES : (lane + 1) * LANES].astype(jnp.float32)
            start += 1


def drain_stage(stage, targets):
    start = 0
    for target in targets:
        for lane in range(target.shape[1] // LANES):
            target[:, lane * LANES : (lane + 1) * LANES] = stage[start].astype(target.dtype)
            start += 1


def as_column(row):
    n = row.shape[1]
    on_diagonal = lax.broadcasted_iota(jnp.int32, (n, n), 0) == lax.broadcasted_iota(
        jnp.int32, (n, n), 1
    )
    return jnp.sum(jnp.where(on_diagonal, row, jnp.zeros_like(row)), axis=1, keepdims=True)


def as_row(column):
    n = column.shape[0]
    on_diagonal = lax.broadcasted_iota(jnp.int32, (n, n), 0) == lax.broadcasted_iota(
        jnp.int32, (n, n), 1
    )
    return jnp.sum(jnp.where(on_diagonal, column, jnp.zeros_like(column)), axis=0, keepdims=True)


def place_kernel(
    blocks,
    capacity,
    owners_outside,
    modules_outside,
    requests_outside,
    sent,
    slots,
    owner_row,
    module_row,
    requests,
    stage,
    done,
):
    rows, width = requests.shape
    piece = width // SUB
    copies = [
        pltpu.make_async_copy(source, target, done.at[number])
        for number, (source, target) in enumerate(
            (
                (owners_outside, owner_row),
                (modules_outside, module_row),
                (requests_outside, requests),
            )
        )
    ]
    for copy in copies:
        copy.start()
    copies[0].wait()
    copies[1].wait()
    modules = module_row[...]
    owners = as_column(owner_row[...])
    named = lax.broadcasted_iota(jnp.int32, (blocks, rows), 0) == modules
    target = jnp.sum(jnp.where(named, owners, 0), axis=0, keepdims=True)
    first = lax.broadcasted_iota(jnp.int32, (rows, rows), 0)
    second = lax.broadcasted_iota(jnp.int32, (rows, rows), 1)
    ahead = (as_column(modules) == modules) & (first < second)
    rank = jnp.sum(ahead.astype(jnp.int32), axis=0, keepdims=True)
    slot_row = rank * blocks + target
    slots[...] = slot_row
    slot_ids = lax.broadcasted_iota(jnp.int32, (capacity * blocks, rows), 0)
    placer = (slot_ids == slot_row).astype(jnp.float32).astype(jnp.bfloat16)
    copies[2].wait()
    for index in range(SUB):
        moved = jnp.dot(
            placer,
            requests[:, index * piece : (index + 1) * piece],
            preferred_element_type=jnp.float32,
        )
        scatter_pieces(stage, index, moved, blocks, capacity, piece)
    drain_stage(stage, (sent,))


def place_more_kernel(blocks, start, capacity, slots, requests, sent, stage):
    rows, width = requests.shape
    piece = width // SUB
    slot_ids = start * blocks + lax.broadcasted_iota(jnp.int32, (capacity * blocks, rows), 0)
    placer = (slot_ids == slots[...]).astype(jnp.float32).astype(jnp.bfloat16)
    for index in range(SUB):
        moved = jnp.dot(
            placer,
            requests[:, index * piece : (index + 1) * piece],
            preferred_element_type=jnp.float32,
        )
        scatter_pieces(stage, index, moved, blocks, capacity, piece)
    drain_stage(stage, (sent,))


def attend_kernel(
    chunks,
    tag_parts,
    tokens,
    w_keys,
    w_values,
    latents,
    slots,
    doc_row,
    partial,
    tokens_in,
    keys_in,
    values_in,
    done,
):
    depth = w_keys.shape[0] // chunks
    copies = []
    for chunk in range(chunks):
        part = pl.ds(chunk * depth, depth)
        copies.append(
            [
                pltpu.make_async_copy(
                    tokens.at[0, :, part], tokens_in.at[chunk], done.at[chunk, 0]
                ),
                pltpu.make_async_copy(w_keys.at[part, :], keys_in.at[chunk], done.at[chunk, 1]),
                pltpu.make_async_copy(w_values.at[part, :], values_in.at[chunk], done.at[chunk, 2]),
            ]
        )
    for group in copies:
        for copy in group:
            copy.start()
    keys = values = 0.0
    for chunk in range(chunks):
        for copy in copies[chunk]:
            copy.wait()
        keys = keys + jnp.dot(
            tokens_in[chunk], keys_in[chunk], preferred_element_type=jnp.float32
        )
        values = values + jnp.dot(
            tokens_in[chunk], values_in[chunk], preferred_element_type=jnp.float32
        )
    latent_count, width = latents.shape
    head_dim = width // HEADS
    queries = latents[...].astype(jnp.bfloat16)
    key_rows = keys.astype(jnp.bfloat16)
    value_rows = values.astype(jnp.bfloat16).astype(jnp.float32)
    peaks, sums = [], []
    for head in range(HEADS):
        lanes = slice(head * head_dim, (head + 1) * head_dim)
        scores = lax.dot_general(
            queries[:, lanes],
            key_rows[:, lanes],
            (((1,), (1,)), ((), ())),
            preferred_element_type=jnp.float32,
        ) / math.sqrt(head_dim)
        peak = jnp.max(scores, axis=1, keepdims=True)
        expo = jnp.exp(scores - peak)
        peaks.append(peak)
        sums.append(jnp.sum(expo, axis=1, keepdims=True))
        partial[head * latent_count : (head + 1) * latent_count, :] = jnp.dot(
            expo,
            value_rows[:, lanes],
            precision=lax.Precision.HIGHEST,
            preferred_element_type=jnp.float32,
        )
    entries = HEADS * latent_count
    partial[entries:, :] = jnp.zeros_like(partial[entries:, :])
    partial[entries : entries + 1, :entries] = as_row(jnp.concatenate(peaks, axis=0))
    partial[entries + 1 : entries + 2, :entries] = as_row(jnp.concatenate(sums, axis=0))
    slot_column = as_column(slots[...])
    documents = as_column(doc_row[...] + 1)
    for part in range(tag_parts):
        lanes = lax.broadcasted_iota(jnp.int32, (slot_column.shape[0], LANES), 1) + part * LANES
        partial[entries + 2 + part : entries + 3 + part, :] = jnp.sum(
            jnp.where(lanes == slot_column, documents, 0), axis=0, keepdims=True
        ).astype(jnp.float32)


def summary_kernel(tag_parts, pieces, latents, w_out, gain, packet):
    members = pieces.shape[0]
    latent_count, width = latents.shape
    entries = HEADS * latent_count
    peaks = [as_column(pieces[c, entries : entries + 1, :entries]) for c in range(members)]
    summit = functools.reduce(jnp.maximum, peaks)
    total, weighted = 0.0, 0.0
    for c in range(members):
        ratio = jnp.exp(peaks[c] - summit)
        total = total + as_column(pieces[c, entries + 1 : entries + 2, :entries]) * ratio
        weighted = weighted + pieces[c, :entries, :] * ratio
    attended = weighted / total
    attended = jnp.concatenate(
        [attended[h * latent_count : (h + 1) * latent_count] for h in range(HEADS)], axis=1
    ).astype(jnp.bfloat16)
    mixed = latents[...] + jnp.dot(attended, w_out[...], preferred_element_type=jnp.float32)
    summary = (
        mixed
        * lax.rsqrt(jnp.mean(mixed * mixed, axis=1, keepdims=True) + 1e-06)
        * gain[...]
    )
    packet[:latent_count, :] = summary.astype(jnp.bfloat16)
    tag_rows = [
        jnp.concatenate(
            [pieces[c, entries + 2 + part : entries + 3 + part, :] for part in range(tag_parts)],
            axis=1,
        )
        for c in range(members)
    ]
    block = jnp.concatenate(tag_rows, axis=0)
    block = jnp.pad(
        block,
        ((0, packet.shape[0] - latent_count - members), (0, width - tag_parts * LANES)),
    )
    packet[latent_count:, :] = block.astype(jnp.bfloat16)


def factor_kernel(
    blocks,
    capacity,
    early,
    latent_count,
    chunks,
    me,
    everyone,
    heads_down,
    heads_up,
    down,
    up,
    tags_first,
    tags_second,
    heads_in,
    factors_out,
    arrived,
    left,
):
    depth = down.shape[1] // chunks
    jobs = []
    for chunk in range(chunks):
        part = pl.ds(chunk * depth, depth)
        for side, (heads, factor) in enumerate(((heads_down, down), (heads_up, up))):
            jobs.append(
                (
                    chunk,
                    side,
                    pltpu.make_async_copy(
                        heads.at[0, :, part], heads_in.at[chunk, side], arrived.at[chunk, side]
                    ),
                    pltpu.make_async_copy(
                        factors_out.at[chunk, side], factor.at[:, part], left.at[chunk, side]
                    ),
                )
            )
    for job in jobs:
        job[2].start()
    documents = everyone.shape[0]
    members = blocks // documents
    summaries = jnp.concatenate([everyone[x, :latent_count, :] for x in range(documents)], axis=0)
    device = me[0, 0]
    my_doc = device // members
    by_entry = jnp.concatenate(
        [everyone[x, latent_count:, :].astype(jnp.float32)[:members] for x in range(documents)],
        axis=0,
    ).astype(jnp.bfloat16)
    source = lax.broadcasted_iota(jnp.int32, (blocks, blocks), 0)
    entry = lax.broadcasted_iota(jnp.int32, (blocks, blocks), 1)
    sorter = source == ((entry // members) ^ my_doc) * members + entry % members
    sorter = sorter.astype(jnp.float32).astype(jnp.bfloat16)
    arranged = jnp.dot(sorter, by_entry, preferred_element_type=jnp.float32)
    lanes = lax.broadcasted_iota(jnp.int32, arranged.shape, 1)
    for slot in range(capacity):
        column = jnp.sum(
            jnp.where(lanes == slot * blocks + device, arranged, 0.0), axis=1, keepdims=True
        ).astype(jnp.int32)
        target, position = (tags_first, slot) if slot < early else (tags_second, slot - early)
        target[position * blocks : (position + 1) * blocks, :] = column
    for chunk, side, arriving, leaving in jobs:
        arriving.wait()
        factors_out[chunk, side] = jnp.dot(
            summaries, heads_in[chunk, side], preferred_element_type=jnp.float32
        ).astype(jnp.bfloat16)
        leaving.start()
    for job in jobs:
        job[3].wait()


def coeff_kernel(blocks, capacity, latent_count, members, me, tags, down, arrived, *refs):
    coeff_out, stage = refs
    coeff_out[...] = coefficients(
        blocks, capacity, latent_count, members, me, tags, down, arrived, stage
    )


def coefficients(
    blocks, capacity, latent_count, members, me, tags, down, arrived, stage
):
    width = down.shape[1]
    piece = width // SUB
    for lane in range(capacity * piece // LANES):
        stage[lane] = arrived[:, lane * LANES : (lane + 1) * LANES].astype(jnp.float32)
    coeff = 0.0
    for index in range(SUB):
        coeff = coeff + lax.dot_general(
            gather_pieces(stage, index, blocks, capacity, piece),
            down[:, index * piece : (index + 1) * piece],
            (((1,), (1,)), ((), ())),
            preferred_element_type=jnp.float32,
        )
    column_doc = (
        lax.broadcasted_iota(jnp.int32, coeff.shape, 1) // latent_count
    ) ^ (me[0, 0] // members)
    matched = tags[...] - 1 == column_doc
    return jnp.where(matched, coeff / math.sqrt(width), 0.0).astype(jnp.bfloat16)


def update_kernel(
    blocks, capacity, latent_count, members, me, tags, down, up, first_coeff, arrived, *refs
):
    update, stage, up_in, up_done = refs
    piece = down.shape[1] // SUB
    late = arrived.shape[1] // piece
    span = down.shape[1] // CHUNKS
    up_copies = [
        pltpu.make_async_copy(
            up.at[:, pl.ds(chunk * span, span)],
            up_in.at[:, pl.ds(chunk * span, span)],
            up_done.at[chunk],
        )
        for chunk in range(CHUNKS)
    ]
    for copy in up_copies:
        copy.start()
    coeff = coefficients(
        blocks, late, latent_count, members, me, tags, down, arrived, stage
    )
    coeff = jnp.concatenate([first_coeff[...], coeff], axis=0)
    for index in range(SUB):
        if index % (SUB // CHUNKS) == 0:
            up_copies[index // (SUB // CHUNKS)].wait()
        moved = jnp.dot(
            coeff, up_in[:, index * piece : (index + 1) * piece], preferred_element_type=jnp.float32
        ) * (1.0 / math.sqrt(latent_count))
        scatter_pieces(stage, index, moved, blocks, capacity, piece)
    drain_stage(stage, (update,))


def finish_kernel(blocks, capacity, returned, slots, requests, adapted, adapted_out, stage, done):
    rows, width = requests.shape
    piece = width // SUB
    fill_stage(stage, (returned,))
    slot_column = as_column(slots[...])
    wanted = lax.broadcasted_iota(jnp.int32, (rows, capacity * blocks), 1) == slot_column
    picker = wanted.astype(jnp.float32).astype(jnp.bfloat16)
    leaving = []
    for index in range(SUB):
        gathered = jnp.dot(
            picker,
            gather_pieces(stage, index, blocks, capacity, piece),
            preferred_element_type=jnp.float32,
        )
        adapted_out[index] = (
            requests[:, index * piece : (index + 1) * piece].astype(jnp.float32) + gathered
        ).astype(adapted.dtype)
        leaving.append(
            pltpu.make_async_copy(
                adapted_out.at[index], adapted.at[:, pl.ds(index * piece, piece)], done.at[index]
            )
        )
        leaving[index].start()
    for copy in leaving:
        copy.wait()


def on_device(
    tokens,
    latents,
    w_keys,
    w_values,
    w_out,
    latent_gain,
    heads_down,
    heads_up,
    owner,
    requests,
    req_doc,
    req_module,
):
    doc_count = lax.axis_size("doc")
    ctx_count = lax.axis_size("ctx")
    blocks = doc_count * ctx_count
    rows, width = requests.shape
    capacity = max(2, rows // blocks + 1)
    piece = width // SUB
    latent_count, latent_width = latents.shape
    head_dim = latent_width // HEADS
    my_doc = lax.axis_index("doc")
    my_ctx = lax.axis_index("ctx")
    early = max(1, (capacity - 1) // 2)
    late = capacity - early
    tag_parts = -(-(capacity * blocks) // LANES)
    me = (my_doc * ctx_count + my_ctx).astype(jnp.int32).reshape(1, 1)
    in_smem = pl.BlockSpec(memory_space=pltpu.SMEM)
    in_vmem = pl.BlockSpec(memory_space=pltpu.VMEM)
    in_hbm = pl.BlockSpec(memory_space=pl.ANY)
    outside = pl.BlockSpec(memory_space=pltpu.HBM)

    def after(values, *others):
        return lax.optimization_barrier((values, *others))[0]

    def block_type(slot_count):
        return jax.ShapeDtypeStruct((blocks * SUB, slot_count * piece), jnp.bfloat16)

    def stage_type(slot_count):
        return pltpu.VMEM((slot_count * piece // LANES, blocks * SUB, LANES), jnp.float32)

    def exchange(values):
        return lax.all_to_all(
            values.reshape(blocks, SUB, -1), ALL, split_axis=0, concat_axis=0, tiled=True
        ).reshape(values.shape)

    first_sent, slots = call(
        functools.partial(place_kernel, blocks, early),
        "place_rows",
        vmem=60,
        in_specs=[outside] * 3,
        out_shape=(
            block_type(early),
            jax.ShapeDtypeStruct((1, rows), jnp.int32),
        ),
        scratch_shapes=[
            pltpu.VMEM((1, blocks), jnp.int32),
            pltpu.VMEM((1, rows), jnp.int32),
            pltpu.VMEM((rows, width), jnp.bfloat16),
            stage_type(early),
            pltpu.SemaphoreType.DMA((3,)),
        ],
    )(
        owner.reshape(1, blocks),
        req_module.reshape(1, rows),
        requests,
    )
    first_arrived = exchange(first_sent)

    token_count = tokens.shape[1]
    entries = HEADS * latent_count
    partial_rows = -(-(entries + 2 + tag_parts) // SUB) * SUB
    chunks = width // (SUB * LANES)
    depth = width // chunks
    partial = call(
        functools.partial(attend_kernel, chunks, tag_parts),
        "attend",
        vmem=60,
        in_specs=[in_hbm] * 3 + [in_vmem] * 3,
        out_shape=jax.ShapeDtypeStruct((partial_rows, head_dim), jnp.float32),
        scratch_shapes=[
            pltpu.VMEM((chunks, token_count, depth), jnp.bfloat16),
            pltpu.VMEM((chunks, depth, latent_width), jnp.bfloat16),
            pltpu.VMEM((chunks, depth, latent_width), jnp.bfloat16),
            pltpu.SemaphoreType.DMA((chunks, 3)),
        ],
    )(tokens, w_keys, w_values, latents, slots, req_doc.reshape(1, rows))
    packet_rows = latent_count + -(-ctx_count // 16) * 16
    packet = call(
        functools.partial(summary_kernel, tag_parts),
        "summarize",
        out_shape=jax.ShapeDtypeStruct((packet_rows, latent_width), jnp.bfloat16),
    )(lax.all_gather(partial, "ctx"), latents, w_out, latent_gain.reshape(1, latent_width))

    share = doc_count // ctx_count
    half = max(1, ctx_count // 2)
    order = [ctx // 2 + ctx % 2 * half for ctx in range(ctx_count)]
    fetched = []
    for turn in range(share):
        pairs = [
            (doc * ctx_count + ctx, (doc ^ (order[ctx] * share + turn)) * ctx_count + ctx)
            for doc in range(doc_count)
            for ctx in range(ctx_count)
        ]
        fetched.append(lax.ppermute(packet, ALL, pairs))
    second_sent = call(
        functools.partial(place_more_kernel, blocks, early, late),
        "place_more",
        vmem=60,
        out_shape=block_type(late),
        scratch_shapes=[stage_type(late)],
    )(after(slots, packet), requests)
    second_arrived = exchange(after(second_sent, *fetched))
    gathered = lax.all_gather(jnp.stack(fetched), "ctx")
    everyone = jnp.stack([gathered[order.index(part)] for part in range(ctx_count)]).reshape(
        doc_count, packet_rows, latent_width
    )

    def tag_type(slot_count):
        return jax.ShapeDtypeStruct((slot_count * blocks, 1), jnp.int32)

    factor_type = jax.ShapeDtypeStruct((doc_count * latent_count, width), jnp.bfloat16)
    long_columns = -(-LONG // (doc_count * latent_count) // LANES) * LANES
    long_type = jax.ShapeDtypeStruct(
        (doc_count * latent_count, max(width, long_columns)), jnp.bfloat16
    )
    down_factor, up_factor, first_tags, second_tags = call(
        functools.partial(factor_kernel, blocks, capacity, early, latent_count, chunks),
        "factors",
        vmem=60,
        in_specs=[in_smem, in_vmem, in_hbm, in_hbm],
        out_specs=(in_hbm, in_hbm, in_vmem, in_vmem),
        out_shape=(factor_type, long_type, tag_type(early), tag_type(late)),
        scratch_shapes=[
            pltpu.VMEM((chunks, 2, latent_width, depth), jnp.bfloat16),
            pltpu.VMEM((chunks, 2, doc_count * latent_count, depth), jnp.bfloat16),
            pltpu.SemaphoreType.DMA((chunks, 2)),
            pltpu.SemaphoreType.DMA((chunks, 2)),
        ],
    )(me, everyone, heads_down, heads_up)

    first_coeff = call(
        functools.partial(coeff_kernel, blocks, early, latent_count, ctx_count),
        "coefficients",
        in_specs=[in_smem] + [in_vmem] * 3,
        out_shape=jax.ShapeDtypeStruct(
            (early * blocks, doc_count * latent_count), jnp.bfloat16
        ),
        scratch_shapes=[stage_type(early)],
    )(me, first_tags, down_factor, first_arrived)
    update = call(
        functools.partial(update_kernel, blocks, capacity, latent_count, ctx_count),
        "update",
        in_specs=[in_smem] + [in_vmem] * 2 + [outside, in_vmem, in_vmem],
        out_shape=block_type(capacity),
        scratch_shapes=[
            stage_type(capacity),
            pltpu.VMEM(factor_type.shape, factor_type.dtype),
            pltpu.SemaphoreType.DMA((CHUNKS,)),
        ],
    )(me, second_tags, down_factor, up_factor, first_coeff, second_arrived)
    returned = exchange(update)
    return call(
        functools.partial(finish_kernel, blocks, capacity),
        "finish_rows",
        out_specs=outside,
        out_shape=jax.ShapeDtypeStruct((rows, width), jnp.bfloat16),
        scratch_shapes=[
            pltpu.VMEM((SUB, rows, piece), jnp.bfloat16),
            stage_type(capacity),
            pltpu.SemaphoreType.DMA((SUB,)),
        ],
    )(returned, slots, requests)


def solution(mesh):
    in_specs = (
        P("doc", "ctx", None),
        P(),
        P(),
        P(),
        P(),
        P(),
        P(ALL, None, None),
        P(ALL, None, None),
        P(),
        P(ALL, None),
        P(ALL),
        P(ALL, None),
    )
    return jax.shard_map(
        on_device, mesh=mesh, in_specs=in_specs, out_specs=P(ALL, None), check_vma=False
    )
```
